512 devices in a mesh: slab: 8 (over x, core), brick: 64 (over y, z).
Axes of the slice: x: 4, y: 8, z: 8, core: 2. Of those that a mesh axis runs over, the one named last changes fastest.
Arguments:
- position: float32 [3, 131072], P(None, ('slab', 'brick')), may hold values from 0 to 1
- orient: float32 [4, 131072], P(None, ('slab', 'brick')), may hold values from -0.5 to 1, as said below
- velocity: float32 [6, 131072], P(None, ('slab', 'brick')), may hold values from -3 to 3
- history: float32 [64, 131072], P(None, ('slab', 'brick')), may hold values from 0 to 1
- template: float32 [3, 64], replicated, may hold values from -1.4 to 1.4
- cross_local: int32 [32768], P(('slab', 'brick')), may hold values from 0 to 255
- cross_ghost: int32 [32768], P(('slab', 'brick')), may hold values from 0 to 511
- cross_count: int32 [512], P(('slab', 'brick')), may hold values from 8 to 64, as said below
- inner_first: int32 [32768], P(('slab', 'brick')), may hold values from 0 to 255
- inner_gap: int32 [32768], P(('slab', 'brick')), may hold values from 1 to 255
- mig_index: int32 [32768], P(('slab', 'brick')), may hold values from 0 to 255, as said below
- mig_dest: int32 [32768, 1], P(('slab', 'brick')), may hold values from 0 to 63; in each aligned block of 64 rows (0 to 63, 64 to 127, ...) at most 2 rows name the same one
Outputs:
- staying: float32 [77, 131072], P(None, ('slab', 'brick'))
- arrivals: float32 [77, 65536], P(None, ('slab', 'brick'))
The draws below stay inside these ranges and needn't reach their ends.
Inputs may be any that keep to these rules, and one draw needn't show every extreme that they name: `orient`: the scalar part lies in 0.6 to 1.0, the other three in -0.5 to 0.5. `cross_count`: at least 8; some brick has exactly 64 in every draw. `mig_index`: 64 distinct clumps of each brick. `mig_dest`: among the 64 migrants of one brick at most 2 go to one destination, and exactly 2 do in some bricks.
All inputs are finite; a program needn't handle non-finite values.
Results may differ from the reference program's by a relative error of at most 0.0003.
Values sent between devices are 32-bit elements; how exact they have to be, the bound alone decides.
No kernel may reach another device: no remote copies, remote signals or barrier semaphores. Data moves between devices by JAX's collectives and lax.ppermute only.
A program may use at most 64 MiB of HBM per device.

```python
import functools
import math
import jax
import jax.numpy as jnp
import numpy as np
from jax import lax

MEMBERS = 64
C_DEV = 256
X_PAIRS = 64
I_PAIRS = 64
SLOT_CAP = 2
MIGRANTS = 64
CLUMPS = 131072
X_TOTAL = 32768
I_TOTAL = 32768
MIG_TOTAL = 32768
SLOTS_TOTAL = 65536
N_SLAB = 8
N_BRICK = 64


def draw_orient(key, part):
    key = jax.random.fold_in(key, 13)
    key_scalar, key_vector = jax.random.split(key)
    scalar = jax.random.uniform(key_scalar, (1, CLUMPS), jnp.float32, 0.6, 1.0)
    vector = jax.random.uniform(key_vector, (3, CLUMPS), jnp.float32, -0.5, 0.5)
    return jnp.concatenate([scalar, vector], 0)


def draw_cross_count(key, part):
    key = jax.random.fold_in(key, 11)
    key_count, key_full = jax.random.split(key)
    devices = N_SLAB * N_BRICK
    counts = jax.random.randint(key_count, (devices,), X_PAIRS // 8, X_PAIRS + 1)
    full_device = jax.random.randint(key_full, (), 0, devices)
    return jnp.where(jnp.arange(devices) == full_device, X_PAIRS, counts).astype(jnp.int32)


def pick_leavers(key_one):
    return jax.random.permutation(key_one, C_DEV)[:MIGRANTS]


def draw_mig_index(key, part):
    key = jax.random.fold_in(key, 12)
    key_list = jax.random.split(key, N_SLAB * N_BRICK)
    picks = jax.vmap(pick_leavers)(key_list)
    return picks.reshape(-1).astype(jnp.int32)


def touch_ends(values, key, smallest, high):
    longest = values.shape.index(max(values.shape))
    spots = []
    for shift in (0, 1):
        where = [jax.random.randint(jax.random.fold_in(key, axis), (), 0, length) for axis, length in enumerate(values.shape)]
        where[longest] = (where[longest] + shift) % values.shape[longest]
        spots.append(tuple(where))
    return values.at[spots[0]].set(smallest).at[spots[1]].set(high)


def steps_of(stream_key, shape, cuts, low, largest):
    loudness = 1.0
    for dim, shards_of in cuts:
        draws = jax.random.uniform(jax.random.fold_in(jax.random.fold_in(stream_key, 6), dim), (shards_of,), jnp.float32, low / len(cuts), largest / len(cuts))
        loudness = loudness * jnp.repeat(jnp.exp(draws), shape[dim] // shards_of).reshape((-1,) + (1,) * (len(shape) - 1 - dim))
    return loudness


def routed_block(rng, own, number, rows, amount, top, bound, skew):
    ranking = jax.random.permutation(rng, amount)
    crowded, usual = portions_of(amount, rows * top, bound, skew, True), portions_of(amount, rows * top, bound, skew, False)
    places = jnp.arange(amount)

    def named(sizes, offset_by):
        used = int((sizes > 0).sum())
        fixed = max(1, used // 4)
        shifted = fixed + (places - fixed + offset_by * (used - fixed)) % max(1, amount - fixed)
        return jnp.zeros((amount,), jnp.int32).at[ranking[jnp.where(places < fixed, places, shifted)]].set(jnp.asarray(sizes, jnp.int32))

    sizes = jnp.where(number % 4 == 0, named(crowded, number // 4), named(usual, number - number // 4 - 1))
    mixed = jax.random.permutation(jax.random.fold_in(own, 3), amount)
    donor, receiver = mixed[0:amount // 2 * 2:2], mixed[1:amount // 2 * 2:2]
    slack = jnp.minimum(sizes[donor] - 1, bound - sizes[receiver]) // 2
    slack = jnp.where((donor == ranking[0]) | (receiver == ranking[0]) | (sizes[receiver] == 0), 0, jnp.maximum(slack, 0))
    shifted = jax.random.randint(jax.random.fold_in(own, 4), (amount // 2,), 0, 1 << 20) % (slack + 1)
    sizes = sizes.at[donor].add(-shifted).at[receiver].add(shifted)
    items = jnp.searchsorted(jnp.cumsum(sizes), jnp.arange(rows * top), side="right").astype(jnp.int32)
    table = items.reshape(top, rows).T
    table = table[jax.random.permutation(jax.random.fold_in(own, 1), rows)]
    offset_by = jax.random.randint(jax.random.fold_in(own, 2), (rows, 1), 0, top)
    return jnp.take_along_axis(table, (jnp.arange(top)[None, :] + offset_by) % top, axis=1)


def portions_of(number_of, total, most, lean, full):
    loads = [(1 << 20) // math.isqrt(rank ** lean) + 1 for rank in range(1, number_of + 1)]
    largest = most if full else min(most, max(-(-total // number_of), total * loads[0] // sum(loads)))
    least = 1 if total - largest >= number_of - 1 else 0
    given, rest = [largest] + [least] * (number_of - 1), total - largest - least * (number_of - 1)
    while rest > 0:
        candidates = [i for i in range(1, number_of) if given[i] < largest] or [i for i in range(1, number_of) if given[i] < most]
        whole, budget = sum([loads[i] for i in candidates]), rest
        for i in candidates:
            addition = min(most - given[i], max(1, budget * loads[i] // whole), rest)
            given[i] = given[i] + addition
            rest = rest - addition
    return np.array(given)


def bell_draw(stream_key, dims, spread, bound, pieces=(), kind=jnp.bfloat16):
    level = steps_of(stream_key, dims, pieces, -0.22, 0.18) if pieces else 1.0
    entries = jax.random.normal(stream_key, dims, jnp.float32) * spread * level
    return jnp.minimum(jnp.maximum(entries, -bound), bound).astype(kind)


def setup_inputs(seed: int = 0) -> dict:
    key_of = jax.random.split(jax.random.key(seed), 13)
    position = jnp.clip(1.0 * jax.random.uniform(key_of[0], (3, CLUMPS), jnp.float32) ** steps_of(key_of[0], (3, CLUMPS), ((1, 512),), -0.2, 0.2), 0.0, 1.0)
    orient = draw_orient(jax.random.fold_in(key_of[12], 71), 0)
    velocity = bell_draw(key_of[2], (6, CLUMPS), 0.5, 3.0, ((1, 512),), jnp.float32)
    history = jnp.clip(1.0 * jax.random.uniform(key_of[3], (MEMBERS, CLUMPS), jnp.float32) ** steps_of(key_of[3], (MEMBERS, CLUMPS), ((1, 512),), -0.2, 0.2), 0.0, 1.0)
    template = bell_draw(key_of[4], (3, MEMBERS), 0.35, 1.4, (), jnp.float32)
    cross_local = touch_ends(jax.random.randint(key_of[5], (X_TOTAL,), 0, C_DEV), jax.random.fold_in(key_of[5], 1), 0, C_DEV - 1).astype(jnp.int32)
    cross_ghost = touch_ends(jax.random.randint(key_of[6], (X_TOTAL,), 0, 2 * C_DEV), jax.random.fold_in(key_of[6], 1), 0, (2 * C_DEV) - 1).astype(jnp.int32)
    cross_count = draw_cross_count(jax.random.fold_in(key_of[12], 71), 0)
    inner_first = touch_ends(jax.random.randint(key_of[8], (I_TOTAL,), 0, C_DEV), jax.random.fold_in(key_of[8], 1), 0, C_DEV - 1).astype(jnp.int32)
    inner_gap = touch_ends(jax.random.randint(key_of[9], (I_TOTAL,), 1, C_DEV), jax.random.fold_in(key_of[9], 1), 1, C_DEV - 1).astype(jnp.int32)
    mig_index = draw_mig_index(jax.random.fold_in(key_of[12], 71), 0)
    mig_dest_keys = jax.random.split(jax.random.fold_in(key_of[11], 1), MIG_TOTAL // MIGRANTS)
    mig_dest_turns = jax.random.permutation(jax.random.fold_in(key_of[11], 3), MIG_TOTAL // MIGRANTS)
    mig_dest = jax.vmap(lambda own, number: routed_block(jax.random.fold_in(key_of[11], 2), own, number, MIGRANTS, N_BRICK, 1, SLOT_CAP, 2))(mig_dest_keys, mig_dest_turns).reshape((MIG_TOTAL, 1))
    return dict(position=position, orient=orient, velocity=velocity, history=history, template=template, cross_local=cross_local, cross_ghost=cross_ghost, cross_count=cross_count, inner_first=inner_first, inner_gap=inner_gap, mig_index=mig_index, mig_dest=mig_dest)


diameter = 0.3
stiffness = 20.0
softening = 0.0001
time_step = 0.02
inertia_scale = 0.05
history_decay = 0.9

def rotation(orient):
    length = jnp.sqrt(lax.optimization_barrier(jnp.sum(orient * orient, axis=0)))
    unit_quat = orient / length
    qw = unit_quat[0]
    qx = unit_quat[1]
    qy = unit_quat[2]
    qz = unit_quat[3]
    matrix_rows = [[1.0 - 2.0 * (qy * qy + qz * qz), 2.0 * (qx * qy - qw * qz), 2.0 * (qx * qz + qw * qy)], [2.0 * (qx * qy + qw * qz), 1.0 - 2.0 * (qx * qx + qz * qz), 2.0 * (qy * qz - qw * qx)], [2.0 * (qx * qz - qw * qy), 2.0 * (qy * qz + qw * qx), 1.0 - 2.0 * (qx * qx + qy * qy)]]
    return jnp.stack([jnp.stack(entry) for entry in matrix_rows])

def arms(orient, template):
    return jnp.einsum('ijc,jm->imc', rotation(orient), template, precision=lax.Precision.HIGHEST)

def contact_block(arm_a, pos_a, hist_a, arm_b, pos_b, hist_b, active):
    place_a = pos_a[:, None, :] + arm_a
    place_b = pos_b[:, None, :] + arm_b
    offset = place_a[:, :, None, :] - place_b[:, None, :, :]
    distance = jnp.sqrt(lax.optimization_barrier(jnp.sum(offset * offset, axis=0)) + softening)
    margin = jnp.maximum(diameter - distance, 0.0) * active
    magnitude = stiffness * margin * (1.0 + 0.5 * (hist_a[:, None, :] + hist_b[None, :, :])) / distance
    pair_push = magnitude[None] * offset
    force_a = lax.optimization_barrier(jnp.sum(pair_push, axis=2))
    force_b = -lax.optimization_barrier(jnp.sum(pair_push, axis=1))
    row_a = jnp.concatenate([lax.optimization_barrier(jnp.sum(force_a, 1)), lax.optimization_barrier(jnp.sum(jnp.cross(arm_a, force_a, axis=0), 1)), lax.optimization_barrier(jnp.sum(margin, 1))], 0)
    row_b = jnp.concatenate([lax.optimization_barrier(jnp.sum(force_b, 1)), lax.optimization_barrier(jnp.sum(jnp.cross(arm_b, force_b, axis=0), 1)), lax.optimization_barrier(jnp.sum(margin, 0))], 0)
    return (row_a, row_b)

def pair_terms(source_a, source_b, index_a, index_b, active, count_a, count_b):
    arm_a_all, pos_a_all, hist_a_all = source_a
    arm_b_all, pos_b_all, hist_b_all = source_b
    pair_total = index_a.shape[0]
    block_size = math.gcd(64, pair_total)
    blocks = pair_total // block_size

    def accumulate(totals_now, block_data):
        sel_a, sel_b, sel_active = block_data
        row_a, row_b = contact_block(arm_a_all[:, :, sel_a], pos_a_all[:, sel_a], hist_a_all[:, sel_a], arm_b_all[:, :, sel_b], pos_b_all[:, sel_b], hist_b_all[:, sel_b], sel_active)
        return ((totals_now[0].at[:, sel_a].add(row_a), totals_now[1].at[:, sel_b].add(row_b)), None)
    starting = (jnp.zeros((70, count_a), jnp.float32), jnp.zeros((70, count_b), jnp.float32))
    totals, unused = lax.scan(accumulate, starting, (index_a.reshape(blocks, block_size), index_b.reshape(blocks, block_size), active.reshape(blocks, block_size)))
    return totals

def advance(position, orient, velocity, history, totals):
    net_force = totals[0:3]
    torque = totals[3:6]
    margin_sum = totals[6:]
    linear = velocity[0:3] + time_step * net_force
    angular = velocity[3:6] + time_step * torque / inertia_scale
    moved_pos = position + time_step * linear
    spin_scalar = -lax.optimization_barrier(jnp.sum(angular * orient[1:4], 0, keepdims=True))
    spin_vector = orient[0:1] * angular + jnp.cross(angular, orient[1:4], axis=0)
    turned = orient + 0.5 * time_step * jnp.concatenate([spin_scalar, spin_vector], 0)
    recalled = history_decay * history + margin_sum
    return jnp.concatenate([moved_pos, turned, linear, angular, recalled], 0)

def depart(new_state, leaving, target, slots_each, bricks):
    moving = leaving.shape[0]
    earlier = jnp.arange(moving)[:, None] > jnp.arange(moving)[None, :]
    same_target = target[:, None] == target[None, :]
    slot_rank = lax.optimization_barrier(jnp.sum((earlier & same_target).astype(jnp.int32), 1))
    column = target * slots_each + slot_rank
    buffer = jnp.zeros((new_state.shape[0], bricks * slots_each), jnp.float32).at[:, column].set(new_state[:, leaving])
    departed = jnp.any(leaving[:, None] == jnp.arange(new_state.shape[1]).astype(jnp.int32)[None, :], 0)
    remaining = jnp.where(departed[None, :], 0.0, new_state)
    return (remaining, buffer)

def reference(position, orient, velocity, history, template, cross_local, cross_ghost, cross_count, inner_first, inner_gap, mig_index, mig_dest):
    devices = N_SLAB * N_BRICK

    def per_device(values_in):
        return values_in.reshape(values_in.shape[0], devices, C_DEV).transpose(1, 0, 2)

    def neighbour(values_in, along, step):
        layout = values_in.reshape((N_SLAB, N_BRICK) + values_in.shape[1:])
        return jnp.roll(layout, step, axis=along).reshape(values_in.shape)
    pos_dev = per_device(position)
    ori_dev = per_device(orient)
    vel_dev = per_device(velocity)
    hist_dev = per_device(history)
    brick_shift = jnp.array([[0.0], [1.0], [0.0]], jnp.float32)
    slab_shift = jnp.array([[1.0], [0.0], [0.0]], jnp.float32)
    far_pos = jnp.concatenate([neighbour(pos_dev, 1, -1) + brick_shift, neighbour(pos_dev, 0, -1) + slab_shift], 2)
    far_ori = jnp.concatenate([neighbour(ori_dev, 1, -1), neighbour(ori_dev, 0, -1)], 2)
    far_hist = jnp.concatenate([neighbour(hist_dev, 1, -1), neighbour(hist_dev, 0, -1)], 2)

    def contacts(inputs):
        pos_here, ori_here, hist_here, pos_far, ori_far, hist_far, local_sel, ghost_sel, pair_count, first_index, gap_index = inputs
        arm_here = arms(ori_here, template)
        arm_far = arms(ori_far, template)
        second = (first_index + gap_index) % C_DEV
        local_set = (arm_here, pos_here, hist_here)
        inner_a, inner_b = pair_terms(local_set, local_set, first_index, second, jnp.ones(first_index.shape, jnp.float32), C_DEV, C_DEV)
        active = (jnp.arange(X_PAIRS) < pair_count).astype(jnp.float32)
        cross_a, far_back = pair_terms(local_set, (arm_far, pos_far, hist_far), local_sel, ghost_sel, active, C_DEV, 2 * C_DEV)
        return (inner_a + inner_b + cross_a, far_back)
    own_rows, back_rows = lax.map(contacts, (pos_dev, ori_dev, hist_dev, far_pos, far_ori, far_hist, cross_local.reshape(devices, X_PAIRS), cross_ghost.reshape(devices, X_PAIRS), cross_count, inner_first.reshape(devices, I_PAIRS), inner_gap.reshape(devices, I_PAIRS)))
    totals = own_rows + neighbour(back_rows[:, :, :C_DEV], 1, 1) + neighbour(back_rows[:, :, C_DEV:], 0, 1)
    states = jax.vmap(advance)(pos_dev, ori_dev, vel_dev, hist_dev, totals)
    leave_fn = functools.partial(depart, slots_each=SLOT_CAP, bricks=N_BRICK)
    remaining, buffer = jax.vmap(leave_fn)(states, mig_index.reshape(devices, MIGRANTS), mig_dest[:, 0].reshape(devices, MIGRANTS))
    staying = remaining.transpose(1, 0, 2).reshape(77, CLUMPS)
    arrivals = buffer.reshape(N_SLAB, N_BRICK, 77, N_BRICK, SLOT_CAP).transpose(2, 0, 3, 1, 4).reshape(77, SLOTS_TOTAL)
    return (staying, arrivals)
```

```python
import jax
import jax.numpy as jnp
from jax import lax
from jax.experimental import pallas as pl
from jax.experimental.pallas import tpu as pltpu
from jax.sharding import PartitionSpec as P

MEMBERS = 64
CLUMPS = 256
LANES = 128
PAIRS = 64
HALF = MEMBERS // 2
SLOT_CAP = 2
IDLE = 1024

DIAMETER = 0.3
SOFTENING = 0.0001
TIME_STEP = 0.02
INERTIA_SCALE = 0.05
HISTORY_DECAY = 0.9

POS = MEMBERS
ORI = MEMBERS + 3
LISTS = MEMBERS + 7
PACKED = MEMBERS + 8

F32 = jnp.float32
BF16 = jnp.bfloat16
I32 = jnp.int32


def parts_of(value):
    high = value.astype(BF16)
    rest = value - high.astype(F32)
    middle = rest.astype(BF16)
    low = (rest - middle.astype(F32)).astype(BF16)
    return (high, middle, low)


def one_hot(index_row, rows=CLUMPS):
    count = lax.broadcasted_iota(I32, (rows, index_row.shape[1]), 0)
    return jnp.where(count == index_row, 1.0, 0.0).astype(F32).astype(BF16)


def gather(parts, chosen):
    high, middle, low = [jnp.dot(part, chosen, preferred_element_type=F32) for part in parts]
    return high + middle + low


def scatter(value, chosen):
    dims = (((1,), (1,)), ((), ()))
    high, middle, low = [
        lax.dot_general(part, chosen, dims, preferred_element_type=F32) for part in parts_of(value)
    ]
    return high + middle + low


def arms_of(picked, template):
    quat = [picked[ORI + k : ORI + k + 1] for k in range(4)]
    scale = lax.rsqrt(quat[0] * quat[0] + quat[1] * quat[1] + quat[2] * quat[2] + quat[3] * quat[3])
    qw, qx, qy, qz = [q * scale for q in quat]
    matrix = [
        [1.0 - 2.0 * (qy * qy + qz * qz), 2.0 * (qx * qy - qw * qz), 2.0 * (qx * qz + qw * qy)],
        [2.0 * (qx * qy + qw * qz), 1.0 - 2.0 * (qx * qx + qz * qz), 2.0 * (qy * qz - qw * qx)],
        [2.0 * (qx * qz - qw * qy), 2.0 * (qy * qz + qw * qx), 1.0 - 2.0 * (qx * qx + qy * qy)],
    ]
    return [row[0] * template[0] + row[1] * template[1] + row[2] * template[2] for row in matrix]


def spread_template(template_ref):
    padded = jnp.concatenate([template_ref[...], jnp.zeros((5, MEMBERS), F32)], 0)
    turned = padded.T
    return [jnp.broadcast_to(turned[:, k : k + 1], (MEMBERS, LANES)) for k in range(3)]


def halves(value):
    lane = lax.broadcasted_iota(I32, (HALF, LANES), 1)
    return jnp.where(lane < PAIRS, value[:HALF], value[HALF:])


def place_source(src_ref, picked, arm, shift):
    for k in range(3):
        src_ref[k] = (picked[POS + k : POS + k + 1] + shift[k]) + arm[k]
    src_ref[3] = 10.0 + 10.0 * picked[0:MEMBERS]


def contact(place, weight, src_ref):
    def step(b, sums):
        other = [src_ref[k, pl.ds(b, 1), :] for k in range(4)]
        dx = place[0] - other[0]
        dy = place[1] - other[1]
        dz = place[2] - other[2]
        square = dx * dx + dy * dy + (dz * dz + SOFTENING)
        inverse = lax.rsqrt(square)
        margin = jnp.maximum(DIAMETER - square * inverse, 0.0)
        push = margin * inverse * (weight + other[3])
        return (sums[0] + push * dx, sums[1] + push * dy, sums[2] + push * dz, sums[3] + margin)

    zero = jnp.zeros((HALF, LANES), F32)
    return lax.fori_loop(0, MEMBERS, step, (zero, zero, zero, zero), unroll=4)


def body_rows(arm, force):
    turn = [
        arm[1] * force[2] - arm[2] * force[1],
        arm[2] * force[0] - arm[0] * force[2],
        arm[0] * force[1] - arm[1] * force[0],
    ]
    return jnp.concatenate(
        [jnp.sum(v, axis=0, keepdims=True) for v in list(force) + turn]
        + [jnp.zeros((2, LANES), F32)],
        0,
    )


def full_batch(picked, template, src_ref):
    arm = arms_of(picked, template)
    weight = 10.0 + 10.0 * picked[0:MEMBERS]
    tail = jnp.zeros((8, LANES), F32)
    margins = []
    for cut in (slice(0, HALF), slice(HALF, MEMBERS)):
        own = [a[cut] for a in arm]
        place = [picked[POS + k : POS + k + 1] + own[k] for k in range(3)]
        out = contact(place, weight[cut], src_ref)
        margins.append(out[3])
        tail = tail + body_rows(own, out[0:3])
    return jnp.concatenate(margins + [tail], 0)


def half_batch(picked, template, src_ref):
    arm = arms_of(picked, [halves(t) for t in template])
    weight = 10.0 + 10.0 * halves(picked[0:MEMBERS])
    place = [picked[POS + k : POS + k + 1] + arm[k] for k in range(3)]
    out = contact(place, weight, src_ref)
    lane = lax.broadcasted_iota(I32, (HALF, LANES), 1)
    lower = jnp.where(lane < PAIRS, out[3], 0.0)
    upper = jnp.where(lane < PAIRS, 0.0, out[3])
    return jnp.concatenate([lower, upper, body_rows(arm, out[0:3])], 0)


def pack_kernel(pos_ref, ori_ref, hist_ref, local_ref, ghost_ref, count_ref, out_ref):
    out_ref[0:MEMBERS] = hist_ref[...]
    slot = lax.broadcasted_iota(I32, (1, PAIRS), 1)
    live = slot < count_ref[0]
    local = local_ref[...].astype(F32)
    code = jnp.where(live, ghost_ref[...], ghost_ref[...] + IDLE).astype(F32)
    lists = jnp.concatenate([local, local, code, code], 1)
    out_ref[MEMBERS:PACKED] = jnp.concatenate([pos_ref[...], ori_ref[...], lists], 0)


def inner_kernel(packed_ref, template_ref, first_ref, gap_ref, out_ref, src_ref):
    template = spread_template(template_ref)
    first = first_ref[...]
    second = jnp.bitwise_and(first + gap_ref[...], CLUMPS - 1)
    target = one_hot(jnp.concatenate([first, second], 1))
    source = one_hot(jnp.concatenate([second, first], 1))
    parts = parts_of(packed_ref[...])
    picked = gather(parts, source)
    place_source(src_ref, picked, arms_of(picked, template), (0.0, 0.0, 0.0))
    rows = full_batch(gather(parts, target), template, src_ref)
    out_ref[...] = scatter(rows, target)


def outer_kernel(
    packed_ref,
    brick_next_ref,
    slab_next_ref,
    brick_back_ref,
    slab_back_ref,
    inner_ref,
    velocity_ref,
    template_ref,
    local_ref,
    ghost_ref,
    count_ref,
    leaving_ref,
    leaving_row_ref,
    target_ref,
    target_row_ref,
    staying_ref,
    buffer_ref,
    src_ref,
):
    template = spread_template(template_ref)
    lane = lax.broadcasted_iota(I32, (1, LANES), 1)
    low = lane < PAIRS
    local = local_ref[...]
    ghost = ghost_ref[...]
    live = lax.broadcasted_iota(I32, (1, PAIRS), 1) < count_ref[0]
    local_code = jnp.where(live, local, local + IDLE)
    local = jnp.concatenate([local, local], 1)
    ghost = jnp.concatenate([ghost, ghost], 1)
    local_code = jnp.concatenate([local_code, local_code], 1)
    brick_lists = brick_back_ref[LISTS : LISTS + 1].astype(I32)
    slab_lists = slab_back_ref[LISTS : LISTS + 1].astype(I32)
    brick_local, brick_code = brick_lists[:, :LANES], brick_lists[:, LANES:]
    slab_local, slab_code = slab_lists[:, :LANES], slab_lists[:, LANES:]

    own = parts_of(packed_ref[...])
    source = (
        gather(parts_of(brick_next_ref[...]), one_hot(jnp.where(low, ghost, -1)))
        + gather(parts_of(slab_next_ref[...]), one_hot(jnp.where(low, ghost - CLUMPS, -1)))
        + gather(parts_of(brick_back_ref[...]), one_hot(jnp.where(low, -1, brick_local)))
    )
    near = ghost < CLUMPS
    shift = (
        jnp.where(low, jnp.where(near, 0.0, 1.0), 0.0),
        jnp.where(low, jnp.where(near, 1.0, 0.0), -1.0),
        0.0,
    )
    place_source(src_ref, source, arms_of(source, template), shift)
    chosen = one_hot(jnp.where(low, local, jnp.bitwise_and(brick_code, CLUMPS - 1)))
    rows = full_batch(gather(own, chosen), template, src_ref)
    totals = inner_ref[...] + scatter(rows, one_hot(jnp.where(low, local_code, brick_code)))

    source = gather(parts_of(slab_back_ref[...]), one_hot(slab_local))
    place_source(src_ref, source, arms_of(source, template), (-1.0, 0.0, 0.0))
    chosen = one_hot(jnp.bitwise_and(slab_code, CLUMPS - 1))
    rows = half_batch(gather(own, chosen), template, src_ref)
    totals = totals + scatter(rows, one_hot(slab_code - CLUMPS))

    state = packed_ref[...]
    velocity = velocity_ref[...]
    orient = [state[ORI + k : ORI + k + 1] for k in range(4)]
    force = totals[MEMBERS : MEMBERS + 3]
    torque = totals[MEMBERS + 3 : MEMBERS + 6]
    linear = velocity[0:3] + TIME_STEP * force
    angular = velocity[3:6] + TIME_STEP * torque / INERTIA_SCALE
    centre = state[POS : POS + 3] + TIME_STEP * linear
    wx, wy, wz = [angular[k : k + 1] for k in range(3)]
    ow, ox, oy, oz = orient
    spin = [
        -(wx * ox + wy * oy + wz * oz),
        ow * wx + (wy * oz - wz * oy),
        ow * wy + (wz * ox - wx * oz),
        ow * wz + (wx * oy - wy * ox),
    ]
    turned = [orient[k] + 0.5 * TIME_STEP * spin[k] for k in range(4)]
    history = HISTORY_DECAY * state[0:MEMBERS] + totals[0:MEMBERS]
    head = jnp.concatenate([centre] + turned + [linear, angular], 0)

    dest = target_row_ref[...]
    order = lax.broadcasted_iota(I32, (PAIRS, PAIRS), 0) < lax.broadcasted_iota(I32, (PAIRS, PAIRS), 1)
    same = jnp.where(order & (target_ref[...] == dest), 1.0, 0.0)
    rank = jnp.sum(same, axis=0, keepdims=True).astype(I32)
    column = one_hot(dest * SLOT_CAP + rank, 64 * SLOT_CAP)
    clump = lax.broadcasted_iota(I32, (PAIRS, CLUMPS), 1)
    leaves = jnp.where(leaving_ref[...] == clump, 1.0, 0.0)
    departed = jnp.sum(leaves, axis=0, keepdims=True) > 0.5
    route = jnp.dot(column, leaves.astype(BF16), preferred_element_type=F32).astype(BF16)
    full = jnp.concatenate([history, head, jnp.zeros((LANES - 77, CLUMPS), F32)], 0)
    buffer_ref[...] = sum(
        lax.dot_general(route, part, (((1,), (1,)), ((), ())), preferred_element_type=F32)
        for part in parts_of(full)
    )
    staying_ref[0:13] = jnp.where(departed, 0.0, head)
    staying_ref[13:77] = jnp.where(departed, 0.0, history)


def turn_kernel(in_ref, out_ref):
    turned = in_ref[...].T
    out_ref[0:13] = turned[MEMBERS : MEMBERS + 13]
    out_ref[13:77] = turned[0:MEMBERS]


def vmem():
    return pl.BlockSpec(memory_space=pltpu.VMEM)


def smem():
    return pl.BlockSpec(memory_space=pltpu.SMEM)


def from_behind(value, axis, steps):
    count = lax.axis_size(axis)
    pairs = [(source, (source + steps) % count) for source in range(count)]
    return lax.ppermute(value, axis, pairs)


def shards(
    position,
    orient,
    velocity,
    history,
    template,
    cross_local,
    cross_ghost,
    cross_count,
    inner_first,
    inner_gap,
    mig_index,
    mig_dest,
):
    row = (1, PAIRS)
    local, ghost = cross_local.reshape(row), cross_ghost.reshape(row)
    packed = pl.pallas_call(
        pack_kernel,
        out_shape=jax.ShapeDtypeStruct((PACKED, CLUMPS), F32),
        in_specs=[vmem()] * 5 + [smem()],
        out_specs=vmem(),
        name="pack",
    )(position, orient, history, local, ghost, cross_count)
    slab_next = from_behind(packed, "slab", -1)
    slab_back = from_behind(packed, "slab", 1)
    brick_next = from_behind(packed, "brick", -1)
    brick_back = from_behind(packed, "brick", 1)
    inner = pl.pallas_call(
        inner_kernel,
        out_shape=jax.ShapeDtypeStruct((PACKED, CLUMPS), F32),
        in_specs=[vmem()] * 4,
        out_specs=vmem(),
        scratch_shapes=[pltpu.VMEM((4, MEMBERS, LANES), F32)],
        cost_estimate=pl.CostEstimate(flops=20_000_000, bytes_accessed=400_000, transcendentals=600_000),
        name="inner",
    )(packed, template, inner_first.reshape(row), inner_gap.reshape(row))
    staying, buffer = pl.pallas_call(
        outer_kernel,
        out_shape=(
            jax.ShapeDtypeStruct((77, CLUMPS), F32),
            jax.ShapeDtypeStruct((64 * SLOT_CAP, LANES), F32),
        ),
        in_specs=[vmem()] * 10 + [smem()] + [vmem()] * 4,
        out_specs=(vmem(), vmem()),
        scratch_shapes=[pltpu.VMEM((4, MEMBERS, LANES), F32)],
        cost_estimate=pl.CostEstimate(flops=30_000_000, bytes_accessed=400_000, transcendentals=800_000),
        name="outer",
    )(
        packed,
        brick_next,
        slab_next,
        brick_back,
        slab_back,
        inner,
        velocity,
        template,
        local,
        ghost,
        cross_count,
        mig_index.reshape(PAIRS, 1),
        mig_index.reshape(row),
        mig_dest,
        mig_dest.reshape(row),
    )
    arrived = lax.all_to_all(buffer.reshape(64, SLOT_CAP, LANES), "brick", split_axis=0, concat_axis=0)
    arrivals = pl.pallas_call(
        turn_kernel,
        out_shape=jax.ShapeDtypeStruct((77, 64 * SLOT_CAP), F32),
        in_specs=[vmem()],
        out_specs=vmem(),
        name="turn",
    )(arrived.reshape(64 * SLOT_CAP, LANES))
    return (staying, arrivals)


def solution(mesh):
    both = ("slab", "brick")
    return jax.shard_map(
        shards,
        mesh=mesh,
        in_specs=(
            P(None, both),
            P(None, both),
            P(None, both),
            P(None, both),
            P(),
            P(both),
            P(both),
            P(both),
            P(both),
            P(both),
            P(both),
            P(both, None),
        ),
        out_specs=(P(None, both), P(None, both)),
        check_vma=False,
    )
```

```python
import jax
import jax.numpy as jnp
from jax import lax
from jax.experimental import pallas as pl
from jax.experimental.pallas import tpu as pltpu
from jax.sharding import PartitionSpec as P

MEMBERS = 64
CLUMPS = 256
LANES = 128
PAIRS = 64
HALF = MEMBERS // 2
SLOT_CAP = 2
VMEM_LIMIT = 4 * 1024 * 1024
IDLE = 1024

DIAMETER = 0.3
SOFTENING = 0.0001
TIME_STEP = 0.02
INERTIA_SCALE = 0.05
HISTORY_DECAY = 0.9

POS = MEMBERS
ORI = MEMBERS + 3
LISTS = MEMBERS + 7
PACKED = MEMBERS + 8

F32 = jnp.float32
BF16 = jnp.bfloat16
I32 = jnp.int32


def parts_of(value):
    high = value.astype(BF16)
    rest = value - high.astype(F32)
    middle = rest.astype(BF16)
    low = (rest - middle.astype(F32)).astype(BF16)
    return (high, middle, low)


def one_hot(index_row, rows=CLUMPS):
    count = lax.broadcasted_iota(I32, (rows, index_row.shape[1]), 0)
    return jnp.where(count == index_row, 1.0, 0.0).astype(F32).astype(BF16)


def gather(parts, chosen):
    high, middle, low = [jnp.dot(part, chosen, preferred_element_type=F32) for part in parts]
    return high + middle + low


def scatter(value, chosen):
    dims = (((1,), (1,)), ((), ()))
    high, middle, low = [
        lax.dot_general(part, chosen, dims, preferred_element_type=F32) for part in parts_of(value)
    ]
    return high + middle + low


def arms_of(picked, template):
    quat = [picked[ORI + k : ORI + k + 1] for k in range(4)]
    scale = lax.rsqrt(quat[0] * quat[0] + quat[1] * quat[1] + quat[2] * quat[2] + quat[3] * quat[3])
    qw, qx, qy, qz = [q * scale for q in quat]
    matrix = [
        [1.0 - 2.0 * (qy * qy + qz * qz), 2.0 * (qx * qy - qw * qz), 2.0 * (qx * qz + qw * qy)],
        [2.0 * (qx * qy + qw * qz), 1.0 - 2.0 * (qx * qx + qz * qz), 2.0 * (qy * qz - qw * qx)],
        [2.0 * (qx * qz - qw * qy), 2.0 * (qy * qz + qw * qx), 1.0 - 2.0 * (qx * qx + qy * qy)],
    ]
    return [row[0] * template[0] + row[1] * template[1] + row[2] * template[2] for row in matrix]


def spread_template(template_ref):
    padded = jnp.concatenate([template_ref[...], jnp.zeros((5, MEMBERS), F32)], 0)
    turned = padded.T
    return [jnp.broadcast_to(turned[:, k : k + 1], (MEMBERS, LANES)) for k in range(3)]


def halves(value):
    lane = lax.broadcasted_iota(I32, (HALF, LANES), 1)
    return jnp.where(lane < PAIRS, value[:HALF], value[HALF:])


def place_source(src_ref, picked, arm, shift):
    for k in range(3):
        src_ref[k] = (picked[POS + k : POS + k + 1] + shift[k]) + arm[k]
    src_ref[3] = 10.0 + 10.0 * picked[0:MEMBERS]


def contact(place, weight, src_ref):
    def step(b, sums):
        other = [src_ref[k, pl.ds(b, 1), :] for k in range(4)]
        dx = place[0] - other[0]
        dy = place[1] - other[1]
        dz = place[2] - other[2]
        square = dx * dx + dy * dy + (dz * dz + SOFTENING)
        inverse = lax.rsqrt(square)
        margin = jnp.maximum(DIAMETER - square * inverse, 0.0)
        push = margin * inverse * (weight + other[3])
        return (sums[0] + push * dx, sums[1] + push * dy, sums[2] + push * dz, sums[3] + margin)

    zero = jnp.zeros((HALF, LANES), F32)
    return lax.fori_loop(0, MEMBERS, step, (zero, zero, zero, zero), unroll=4)


def body_rows(arm, force):
    turn = [
        arm[1] * force[2] - arm[2] * force[1],
        arm[2] * force[0] - arm[0] * force[2],
        arm[0] * force[1] - arm[1] * force[0],
    ]
    return jnp.concatenate(
        [jnp.sum(v, axis=0, keepdims=True) for v in list(force) + turn]
        + [jnp.zeros((2, LANES), F32)],
        0,
    )


def full_batch(picked, template, src_ref):
    arm = arms_of(picked, template)
    weight = 10.0 + 10.0 * picked[0:MEMBERS]
    tail = jnp.zeros((8, LANES), F32)
    margins = []
    for cut in (slice(0, HALF), slice(HALF, MEMBERS)):
        own = [a[cut] for a in arm]
        place = [picked[POS + k : POS + k + 1] + own[k] for k in range(3)]
        out = contact(place, weight[cut], src_ref)
        margins.append(out[3])
        tail = tail + body_rows(own, out[0:3])
    return jnp.concatenate(margins + [tail], 0)


def half_batch(picked, template, src_ref):
    arm = arms_of(picked, [halves(t) for t in template])
    weight = 10.0 + 10.0 * halves(picked[0:MEMBERS])
    place = [picked[POS + k : POS + k + 1] + arm[k] for k in range(3)]
    out = contact(place, weight, src_ref)
    lane = lax.broadcasted_iota(I32, (HALF, LANES), 1)
    lower = jnp.where(lane < PAIRS, out[3], 0.0)
    upper = jnp.where(lane < PAIRS, 0.0, out[3])
    return jnp.concatenate([lower, upper, body_rows(arm, out[0:3])], 0)


def pack_kernel(pos_ref, ori_ref, hist_ref, local_ref, ghost_ref, count_ref, out_ref):
    out_ref[0:MEMBERS] = hist_ref[...]
    slot = lax.broadcasted_iota(I32, (1, PAIRS), 1)
    live = slot < count_ref[0]
    local = local_ref[...].astype(F32)
    code = jnp.where(live, ghost_ref[...], ghost_ref[...] + IDLE).astype(F32)
    lists = jnp.concatenate([local, local, code, code], 1)
    out_ref[MEMBERS:PACKED] = jnp.concatenate([pos_ref[...], ori_ref[...], lists], 0)


def routes(leaving, dest):
    to = one_hot(dest, 64)
    before = lax.broadcasted_iota(I32, (PAIRS, PAIRS), 0) < lax.broadcasted_iota(I32, (PAIRS, PAIRS), 1)
    before = jnp.where(before, 1.0, 0.0).astype(BF16)
    earlier = jnp.dot(to, before, preferred_element_type=F32)
    rank = jnp.sum(earlier * to.astype(F32), axis=0, keepdims=True).astype(I32)
    column = one_hot(dest * SLOT_CAP + rank, 64 * SLOT_CAP)
    leaves = one_hot(leaving)
    dims = (((1,), (1,)), ((), ()))
    route = lax.dot_general(column, leaves, dims, preferred_element_type=F32)
    ones = jnp.ones((8, PAIRS), F32).astype(BF16)
    return route, lax.dot_general(ones, leaves, dims, preferred_element_type=F32)


def inner_kernel(
    packed_ref,
    template_ref,
    first_ref,
    gap_ref,
    leaving_ref,
    dest_ref,
    out_ref,
    route_ref,
    departed_ref,
    src_ref,
):
    route_ref[...], departed_ref[...] = routes(leaving_ref[...], dest_ref[...])
    template = spread_template(template_ref)
    first = first_ref[...]
    second = jnp.bitwise_and(first + gap_ref[...], CLUMPS - 1)
    target = one_hot(jnp.concatenate([first, second], 1))
    source = one_hot(jnp.concatenate([second, first], 1))
    parts = parts_of(packed_ref[...])
    picked = gather(parts, source)
    place_source(src_ref, picked, arms_of(picked, template), (0.0, 0.0, 0.0))
    rows = full_batch(gather(parts, target), template, src_ref)
    out_ref[...] = scatter(rows, target)


def outer_kernel(
    packed_ref,
    brick_next_ref,
    slab_next_ref,
    brick_back_ref,
    slab_back_ref,
    inner_ref,
    velocity_ref,
    template_ref,
    local_ref,
    ghost_ref,
    count_ref,
    route_ref,
    departed_ref,
    staying_ref,
    buffer_ref,
    src_ref,
):
    template = spread_template(template_ref)
    lane = lax.broadcasted_iota(I32, (1, LANES), 1)
    low = lane < PAIRS
    local = local_ref[...]
    ghost = ghost_ref[...]
    live = lax.broadcasted_iota(I32, (1, PAIRS), 1) < count_ref[0]
    local_code = jnp.where(live, local, local + IDLE)
    local = jnp.concatenate([local, local], 1)
    ghost = jnp.concatenate([ghost, ghost], 1)
    local_code = jnp.concatenate([local_code, local_code], 1)
    brick_lists = brick_back_ref[LISTS : LISTS + 1].astype(I32)
    slab_lists = slab_back_ref[LISTS : LISTS + 1].astype(I32)
    brick_local, brick_code = brick_lists[:, :LANES], brick_lists[:, LANES:]
    slab_local, slab_code = slab_lists[:, :LANES], slab_lists[:, LANES:]

    own = parts_of(packed_ref[...])
    source = (
        gather(parts_of(brick_next_ref[...]), one_hot(jnp.where(low, ghost, -1)))
        + gather(parts_of(slab_next_ref[...]), one_hot(jnp.where(low, ghost - CLUMPS, -1)))
        + gather(parts_of(brick_back_ref[...]), one_hot(jnp.where(low, -1, brick_local)))
    )
    near = ghost < CLUMPS
    shift = (
        jnp.where(low, jnp.where(near, 0.0, 1.0), 0.0),
        jnp.where(low, jnp.where(near, 1.0, 0.0), -1.0),
        0.0,
    )
    place_source(src_ref, source, arms_of(source, template), shift)
    chosen = one_hot(jnp.where(low, local, jnp.bitwise_and(brick_code, CLUMPS - 1)))
    rows = full_batch(gather(own, chosen), template, src_ref)
    totals = inner_ref[...] + scatter(rows, one_hot(jnp.where(low, local_code, brick_code)))

    source = gather(parts_of(slab_back_ref[...]), one_hot(slab_local))
    place_source(src_ref, source, arms_of(source, template), (-1.0, 0.0, 0.0))
    chosen = one_hot(jnp.bitwise_and(slab_code, CLUMPS - 1))
    rows = half_batch(gather(own, chosen), template, src_ref)
    totals = totals + scatter(rows, one_hot(slab_code - CLUMPS))

    state = packed_ref[...]
    velocity = velocity_ref[...]
    orient = [state[ORI + k : ORI + k + 1] for k in range(4)]
    force = totals[MEMBERS : MEMBERS + 3]
    torque = totals[MEMBERS + 3 : MEMBERS + 6]
    linear = velocity[0:3] + TIME_STEP * force
    angular = velocity[3:6] + TIME_STEP * torque / INERTIA_SCALE
    centre = state[POS : POS + 3] + TIME_STEP * linear
    wx, wy, wz = [angular[k : k + 1] for k in range(3)]
    ow, ox, oy, oz = orient
    spin = [
        -(wx * ox + wy * oy + wz * oz),
        ow * wx + (wy * oz - wz * oy),
        ow * wy + (wz * ox - wx * oz),
        ow * wz + (wx * oy - wy * ox),
    ]
    turned = [orient[k] + 0.5 * TIME_STEP * spin[k] for k in range(4)]
    history = HISTORY_DECAY * state[0:MEMBERS] + totals[0:MEMBERS]
    head = jnp.concatenate([centre] + turned + [linear, angular], 0)

    departed = departed_ref[0:1] > 0.5
    route = route_ref[...].astype(BF16)
    full = jnp.concatenate([history, head, jnp.zeros((LANES - 77, CLUMPS), F32)], 0)
    buffer_ref[...] = sum(
        lax.dot_general(route, part, (((1,), (1,)), ((), ())), preferred_element_type=F32)
        for part in parts_of(full)
    )
    staying_ref[0:13] = jnp.where(departed, 0.0, head)
    staying_ref[13:77] = jnp.where(departed, 0.0, history)


def turn_kernel(in_ref, out_ref):
    turned = in_ref[...].T
    out_ref[0:13] = turned[MEMBERS : MEMBERS + 13]
    out_ref[13:77] = turned[0:MEMBERS]


def vmem():
    return pl.BlockSpec(memory_space=pltpu.VMEM)


def small():
    return pltpu.CompilerParams(vmem_limit_bytes=VMEM_LIMIT)


def smem():
    return pl.BlockSpec(memory_space=pltpu.SMEM)


def from_behind(value, axis, steps):
    count = lax.axis_size(axis)
    pairs = [(source, (source + steps) % count) for source in range(count)]
    return lax.ppermute(value, axis, pairs)


def shards(
    position,
    orient,
    velocity,
    history,
    template,
    cross_local,
    cross_ghost,
    cross_count,
    inner_first,
    inner_gap,
    mig_index,
    mig_dest,
):
    row = (1, PAIRS)
    local, ghost = cross_local.reshape(row), cross_ghost.reshape(row)
    packed = pl.pallas_call(
        pack_kernel,
        out_shape=jax.ShapeDtypeStruct((PACKED, CLUMPS), F32),
        in_specs=[vmem()] * 5 + [smem()],
        out_specs=vmem(),
        compiler_params=small(),
        name="pack",
    )(position, orient, history, local, ghost, cross_count)
    slab_next = from_behind(packed, "slab", -1)
    slab_back = from_behind(packed, "slab", 1)
    brick_next = from_behind(packed, "brick", -1)
    brick_back = from_behind(packed, "brick", 1)
    inner, route, departed = pl.pallas_call(
        inner_kernel,
        out_shape=(
            jax.ShapeDtypeStruct((PACKED, CLUMPS), F32),
            jax.ShapeDtypeStruct((64 * SLOT_CAP, CLUMPS), F32),
            jax.ShapeDtypeStruct((8, CLUMPS), F32),
        ),
        in_specs=[vmem()] * 6,
        out_specs=(vmem(),) * 3,
        scratch_shapes=[pltpu.VMEM((4, MEMBERS, LANES), F32)],
        cost_estimate=pl.CostEstimate(flops=20_000_000, bytes_accessed=400_000, transcendentals=600_000),
        compiler_params=small(),
        name="inner",
    )(
        packed,
        template,
        inner_first.reshape(row),
        inner_gap.reshape(row),
        mig_index.reshape(row),
        mig_dest.reshape(row),
    )
    staying, buffer = pl.pallas_call(
        outer_kernel,
        out_shape=(
            jax.ShapeDtypeStruct((77, CLUMPS), F32),
            jax.ShapeDtypeStruct((64 * SLOT_CAP, LANES), F32),
        ),
        in_specs=[vmem()] * 10 + [smem()] + [vmem()] * 2,
        out_specs=(vmem(), vmem()),
        scratch_shapes=[pltpu.VMEM((4, MEMBERS, LANES), F32)],
        cost_estimate=pl.CostEstimate(flops=30_000_000, bytes_accessed=400_000, transcendentals=800_000),
        compiler_params=small(),
        name="outer",
    )(
        packed,
        brick_next,
        slab_next,
        brick_back,
        slab_back,
        inner,
        velocity,
        template,
        local,
        ghost,
        cross_count,
        route,
        departed,
    )
    arrived = lax.all_to_all(buffer.reshape(64, SLOT_CAP, LANES), "brick", split_axis=0, concat_axis=0)
    arrivals = pl.pallas_call(
        turn_kernel,
        out_shape=jax.ShapeDtypeStruct((77, 64 * SLOT_CAP), F32),
        in_specs=[vmem()],
        out_specs=vmem(),
        compiler_params=small(),
        name="turn",
    )(arrived.reshape(64 * SLOT_CAP, LANES))
    return (staying, arrivals)


def solution(mesh):
    both = ("slab", "brick")
    return jax.shard_map(
        shards,
        mesh=mesh,
        in_specs=(
            P(None, both),
            P(None, both),
            P(None, both),
            P(None, both),
            P(),
            P(both),
            P(both),
            P(both),
            P(both),
            P(both),
            P(both),
            P(both, None),
        ),
        out_specs=(P(None, both), P(None, both)),
        check_vma=False,
    )
```

```python
import jax
import jax.numpy as jnp
from jax import lax
from jax.experimental import pallas as pl
from jax.experimental.pallas import tpu as pltpu
from jax.sharding import PartitionSpec as P

MEMBERS = 64
CLUMPS = 256
LANES = 128
PAIRS = 64
HALF = MEMBERS // 2
SLOT_CAP = 2
BRICKS = 64
CHUNK = 2 * SLOT_CAP
VMEM_LIMIT = 8 * 1024 * 1024
IDLE = 1024

DIAMETER = 0.3
SOFTENING = 0.0001
TIME_STEP = 0.02
INERTIA_SCALE = 0.05
HISTORY_DECAY = 0.9

POS = MEMBERS
ORI = MEMBERS + 3
LISTS = MEMBERS + 7
PACKED = MEMBERS + 8

F32 = jnp.float32
BF16 = jnp.bfloat16
I32 = jnp.int32


def parts_of(value):
    high = value.astype(BF16)
    rest = value - high.astype(F32)
    middle = rest.astype(BF16)
    low = (rest - middle.astype(F32)).astype(BF16)
    return (high, middle, low)


def one_hot(index_row, rows=CLUMPS):
    count = lax.broadcasted_iota(I32, (rows, index_row.shape[1]), 0)
    return jnp.where(count == index_row, 1.0, 0.0).astype(F32).astype(BF16)


def gather(parts, chosen):
    high, middle, low = [jnp.dot(part, chosen, preferred_element_type=F32) for part in parts]
    return high + middle + low


def scatter(value, chosen):
    dims = (((1,), (1,)), ((), ()))
    high, middle, low = [
        lax.dot_general(part, chosen, dims, preferred_element_type=F32) for part in parts_of(value)
    ]
    return high + middle + low


def arms_of(picked, template):
    quat = [picked[ORI + k : ORI + k + 1] for k in range(4)]
    scale = lax.rsqrt(quat[0] * quat[0] + quat[1] * quat[1] + quat[2] * quat[2] + quat[3] * quat[3])
    qw, qx, qy, qz = [q * scale for q in quat]
    matrix = [
        [1.0 - 2.0 * (qy * qy + qz * qz), 2.0 * (qx * qy - qw * qz), 2.0 * (qx * qz + qw * qy)],
        [2.0 * (qx * qy + qw * qz), 1.0 - 2.0 * (qx * qx + qz * qz), 2.0 * (qy * qz - qw * qx)],
        [2.0 * (qx * qz - qw * qy), 2.0 * (qy * qz + qw * qx), 1.0 - 2.0 * (qx * qx + qy * qy)],
    ]
    return [row[0] * template[0] + row[1] * template[1] + row[2] * template[2] for row in matrix]


def spread_template(template_ref):
    padded = jnp.concatenate([template_ref[...], jnp.zeros((5, MEMBERS), F32)], 0)
    turned = padded.T
    return [jnp.broadcast_to(turned[:, k : k + 1], (MEMBERS, LANES)) for k in range(3)]


def twice(row):
    return jnp.concatenate([row, row], 1)


def halves(value):
    lane = lax.broadcasted_iota(I32, (HALF, LANES), 1)
    return jnp.where(lane < PAIRS, value[:HALF], value[HALF:])


def place_source(src_ref, picked, arm, shift):
    for k in range(3):
        src_ref[k] = (picked[POS + k : POS + k + 1] + shift[k]) + arm[k]
    src_ref[3] = 10.0 + 10.0 * picked[0:MEMBERS]


def contact(place, weight, src_ref):
    def step(b, sums):
        other = [src_ref[k, pl.ds(b, 1), :] for k in range(4)]
        dx = place[0] - other[0]
        dy = place[1] - other[1]
        dz = place[2] - other[2]
        square = dx * dx + dy * dy + (dz * dz + SOFTENING)
        inverse = lax.rsqrt(square)
        margin = jnp.maximum(DIAMETER - square * inverse, 0.0)
        push = margin * inverse * (weight + other[3])
        return (sums[0] + push * dx, sums[1] + push * dy, sums[2] + push * dz, sums[3] + margin)

    zero = jnp.zeros((HALF, LANES), F32)
    return lax.fori_loop(0, MEMBERS, step, (zero, zero, zero, zero), unroll=4)


def body_rows(arm, force):
    turn = [
        arm[1] * force[2] - arm[2] * force[1],
        arm[2] * force[0] - arm[0] * force[2],
        arm[0] * force[1] - arm[1] * force[0],
    ]
    return jnp.concatenate(
        [jnp.sum(v, axis=0, keepdims=True) for v in list(force) + turn]
        + [jnp.zeros((2, LANES), F32)],
        0,
    )


def full_batch(picked, template, src_ref):
    arm = arms_of(picked, template)
    weight = 10.0 + 10.0 * picked[0:MEMBERS]
    tail = jnp.zeros((8, LANES), F32)
    margins = []
    for cut in (slice(0, HALF), slice(HALF, MEMBERS)):
        own = [a[cut] for a in arm]
        place = [picked[POS + k : POS + k + 1] + own[k] for k in range(3)]
        out = contact(place, weight[cut], src_ref)
        margins.append(out[3])
        tail = tail + body_rows(own, out[0:3])
    return jnp.concatenate(margins + [tail], 0)


def half_targets(picked, template):
    arm = arms_of(picked, [halves(t) for t in template])
    weight = 10.0 + 10.0 * halves(picked[0:MEMBERS])
    place = [picked[POS + k : POS + k + 1] + arm[k] for k in range(3)]
    return place, weight, arm


def half_rows(arm, out):
    lane = lax.broadcasted_iota(I32, (HALF, LANES), 1)
    lower = jnp.where(lane < PAIRS, out[3], 0.0)
    upper = jnp.where(lane < PAIRS, 0.0, out[3])
    return jnp.concatenate([lower, upper, body_rows(arm, out[0:3])], 0)


def contact_both(place, weight, src_ref, acc_ref):
    def step(b, sums):
        other = [src_ref[k, pl.ds(b, 1), :] for k in range(4)]
        offset = [place[k] - other[k] for k in range(3)]
        square = offset[0] * offset[0] + offset[1] * offset[1] + (offset[2] * offset[2] + SOFTENING)
        inverse = lax.rsqrt(square)
        margin = jnp.maximum(DIAMETER - square * inverse, 0.0)
        push = margin * inverse * (weight + other[3])
        terms = [push * d for d in offset] + [margin]
        for k in range(4):
            acc_ref[k, pl.ds(pl.multiple_of(b * 8, 8), 8), :] = jnp.sum(terms[k].reshape(HALF // 8, 8, LANES), axis=0)
        return tuple(total + term for total, term in zip(sums, terms))

    zero = jnp.zeros((HALF, LANES), F32)
    return lax.fori_loop(0, MEMBERS, step, (zero, zero, zero, zero), unroll=4)


def source_sums(acc_ref):
    out = []
    for k in range(4):
        rows = [acc_ref[k, pl.ds(r, MEMBERS, stride=8), :] for r in range(8)]
        out.append(((rows[0] + rows[1]) + (rows[2] + rows[3])) + ((rows[4] + rows[5]) + (rows[6] + rows[7])))
    return out


def routes(leaving, dest, first_row):
    to = one_hot(dest, BRICKS)
    before = lax.broadcasted_iota(I32, (PAIRS, PAIRS), 0) < lax.broadcasted_iota(I32, (PAIRS, PAIRS), 1)
    before = jnp.where(before, 1.0, 0.0).astype(BF16)
    earlier = jnp.dot(to, before, preferred_element_type=F32)
    rank = jnp.sum(earlier * to.astype(F32), axis=0, keepdims=True).astype(I32)
    return one_hot(dest * CHUNK + first_row + rank, BRICKS * CHUNK), one_hot(leaving)


def spin(angular, orient):
    wx, wy, wz = [angular[k : k + 1] for k in range(3)]
    ow, ox, oy, oz = orient
    return [
        -(wx * ox + wy * oy + wz * oz),
        ow * wx + (wy * oz - wz * oy),
        ow * wy + (wz * ox - wx * oz),
        ow * wz + (wx * oy - wy * ox),
    ]


def change_of(totals, orient):
    linear = TIME_STEP * totals[MEMBERS : MEMBERS + 3]
    angular = TIME_STEP * totals[MEMBERS + 3 : MEMBERS + 6] / INERTIA_SCALE
    turned = [0.5 * TIME_STEP * part for part in spin(angular, orient)]
    return jnp.concatenate([TIME_STEP * linear] + turned + [linear, angular], 0), totals[0:MEMBERS]


def orient_of(packed):
    return [packed[ORI + k : ORI + k + 1] for k in range(4)]


def to_slots(route, rows):
    dims = (((1,), (1,)), ((), ()))
    high, middle, low = [
        lax.dot_general(route, part, dims, preferred_element_type=F32) for part in parts_of(rows)
    ]
    return high + middle + low


def padded(head, history):
    return jnp.concatenate([history, head, jnp.zeros((LANES - 77, head.shape[1]), F32)], 0)


def pack_kernel(
    pos_hbm,
    ori_hbm,
    hist_hbm,
    velocity_hbm,
    template_hbm,
    local_hbm,
    ghost_hbm,
    first_hbm,
    gap_hbm,
    leaving_hbm,
    dest_hbm,
    count_ref,
    packed_ref,
    velocity_ref,
    template_ref,
    local_ref,
    ghost_ref,
    first_ref,
    gap_ref,
    leaving_ref,
    dest_ref,
    pos_ref,
    ori_ref,
    sems,
):
    moves = [
        (hist_hbm, packed_ref.at[0:MEMBERS]),
        (pos_hbm, pos_ref),
        (ori_hbm, ori_ref),
        (local_hbm, local_ref),
        (ghost_hbm, ghost_ref),
        (leaving_hbm, leaving_ref),
        (dest_hbm, dest_ref),
        (velocity_hbm, velocity_ref),
        (template_hbm, template_ref),
        (first_hbm, first_ref),
        (gap_hbm, gap_ref),
    ]
    copies = [pltpu.make_async_copy(a, b, sems.at[k]) for k, (a, b) in enumerate(moves)]
    for copy in copies:
        copy.start()
    for copy in copies[1:]:
        copy.wait()
    live = lax.broadcasted_iota(I32, (1, PAIRS), 1) < count_ref[0]
    ghost = ghost_ref[...]
    code = jnp.where(live, ghost, ghost + IDLE)
    lists = jnp.concatenate([local_ref[...], code, leaving_ref[...], dest_ref[...]], 1).astype(F32)
    packed_ref[MEMBERS:PACKED] = jnp.concatenate([pos_ref[...], ori_ref[...], lists], 0)
    copies[0].wait()


def inner_kernel(
    packed_ref,
    template_ref,
    first_ref,
    gap_ref,
    leaving_ref,
    dest_ref,
    local_ref,
    totals_ref,
    route_ref,
    departed_ref,
    spread_ref,
    target_ref,
    src_ref,
):
    template = spread_template(template_ref)
    for k in range(3):
        spread_ref[k] = template[k]
    column, leaves = routes(leaving_ref[...], dest_ref[...], 0)
    dims = (((1,), (1,)), ((), ()))
    route_ref[...] = lax.dot_general(column, leaves, dims, preferred_element_type=F32)
    ones = jnp.ones((8, PAIRS), F32).astype(BF16)
    departed_ref[...] = lax.dot_general(ones, leaves, dims, preferred_element_type=F32)

    own = parts_of(packed_ref[...])
    place, weight, arm = half_targets(gather(own, one_hot(twice(local_ref[...]))), template)
    for k in range(3):
        target_ref[k] = place[k]
        target_ref[4 + k] = arm[k]
    target_ref[3] = weight

    first = first_ref[...]
    second = jnp.bitwise_and(first + gap_ref[...], CLUMPS - 1)
    target = one_hot(jnp.concatenate([first, second], 1))
    source = one_hot(jnp.concatenate([second, first], 1))
    picked = gather(own, source)
    place_source(src_ref, picked, arms_of(picked, template), (0.0, 0.0, 0.0))
    rows = full_batch(gather(own, target), template, src_ref)
    totals_ref[...] = scatter(rows, target)


def slab_kernel(packed_ref, back_ref, next_ref, inner_ref, spread_ref, ghost_ref, totals_ref, picked_ref, src_ref):
    template = [spread_ref[k] for k in range(3)]
    lists = back_ref[LISTS : LISTS + 1].astype(I32)
    local, code = twice(lists[:, 0:PAIRS]), twice(lists[:, PAIRS : 2 * PAIRS])
    picked_ref[...] = gather(parts_of(next_ref[...]), one_hot(twice(ghost_ref[...]) - CLUMPS))
    source = gather(parts_of(back_ref[...]), one_hot(local))
    place_source(src_ref, source, arms_of(source, template), (-1.0, 0.0, 0.0))
    chosen = one_hot(jnp.bitwise_and(code, CLUMPS - 1))
    place, weight, arm = half_targets(gather(parts_of(packed_ref[...]), chosen), template)
    rows = half_rows(arm, contact(place, weight, src_ref))
    totals_ref[...] = inner_ref[...] + scatter(rows, one_hot(code - CLUMPS))


def brick_kernel(
    packed_ref,
    next_ref,
    picked_ref,
    totals_ref,
    velocity_ref,
    spread_ref,
    target_ref,
    local_ref,
    ghost_ref,
    count_ref,
    route_ref,
    state_ref,
    back_ref,
    buffer_ref,
    src_ref,
    acc_ref,
):
    template = [spread_ref[k] for k in range(3)]
    live = lax.broadcasted_iota(I32, (1, PAIRS), 1) < count_ref[0]
    local = twice(jnp.where(live, local_ref[...], IDLE))
    ghost = twice(ghost_ref[...])
    near = ghost < CLUMPS
    near_live = twice(jnp.where(live, ghost_ref[...], IDLE))

    picked = picked_ref[...] + gather(parts_of(next_ref[...]), one_hot(ghost))
    shift = (jnp.where(near, 0.0, 1.0), jnp.where(near, 1.0, 0.0), 0.0)
    arm_b = arms_of(picked, template)
    place_source(src_ref, picked, arm_b, shift)
    lists = next_ref[LISTS : LISTS + 1].astype(I32)
    column, leaves = routes(lists[:, 2 * PAIRS : 3 * PAIRS], lists[:, 3 * PAIRS :], SLOT_CAP)
    ghosts = one_hot(near_live)
    moving = lax.dot_general(leaves, ghosts, (((0,), (0,)), ((), ())), preferred_element_type=F32)
    moving = jnp.dot(column, moving.astype(BF16), preferred_element_type=F32).astype(BF16)

    out = contact_both([target_ref[k] for k in range(3)], target_ref[3], src_ref, acc_ref)
    rows = half_rows([target_ref[4 + k] for k in range(3)], out)
    totals = totals_ref[...] + scatter(rows, one_hot(local))
    force_x, force_y, force_z, margin = source_sums(acc_ref)
    rows = jnp.concatenate([margin, -body_rows(arm_b, (force_x, force_y, force_z))], 0)
    back_ref[...] = scatter(rows, ghosts)

    state = packed_ref[...]
    head, history = change_of(totals, orient_of(state))
    velocity = velocity_ref[...]
    start = jnp.concatenate([state[POS : POS + 3] + TIME_STEP * velocity[0:3], state[ORI : ORI + 4], velocity], 0)
    drift = [0.5 * TIME_STEP * part for part in spin(velocity[3:6], orient_of(state))]
    nothing = jnp.zeros((3, CLUMPS), F32)
    head = head + start + jnp.concatenate([nothing] + drift + [nothing, nothing], 0)
    full = padded(head, HISTORY_DECAY * state[0:MEMBERS] + history)
    state_ref[...] = full
    head, history = change_of(rows, orient_of(picked))
    buffer_ref[...] = to_slots(route_ref[...].astype(BF16), full) + to_slots(moving, padded(head, history))


def stay_kernel(state_ref, packed_ref, back_ref, departed_ref, staying_ref):
    departed = departed_ref[0:1] > 0.5
    head, history = change_of(back_ref[...], orient_of(packed_ref[...]))
    staying_ref[0:13] = jnp.where(departed, 0.0, state_ref[MEMBERS : MEMBERS + 13] + head)
    staying_ref[13:77] = jnp.where(departed, 0.0, state_ref[0:MEMBERS] + history)


def turn_kernel(in_ref, out_ref, row_ref):
    for slot in range(SLOT_CAP):
        own = in_ref[pl.ds(slot, BRICKS, stride=CHUNK), :]
        more = in_ref[pl.ds(SLOT_CAP + slot, BRICKS, stride=CHUNK), :]
        more = jnp.concatenate([more[BRICKS - 1 :], more[: BRICKS - 1]], 0)
        row_ref[pl.ds(slot, BRICKS, stride=SLOT_CAP), :] = own + more
    turned = row_ref[...].T
    out_ref[0:13] = turned[MEMBERS : MEMBERS + 13]
    out_ref[13:77] = turned[0:MEMBERS]


def vmem():
    return pl.BlockSpec(memory_space=pltpu.VMEM)


def smem():
    return pl.BlockSpec(memory_space=pltpu.SMEM)


def hbm():
    return pl.BlockSpec(memory_space=pltpu.HBM)


def small():
    return pltpu.CompilerParams(vmem_limit_bytes=VMEM_LIMIT)


def cost(flops):
    return pl.CostEstimate(flops=flops, bytes_accessed=400_000, transcendentals=flops // 30)


def array(*shape, dtype=F32):
    return jax.ShapeDtypeStruct(shape, dtype)


def from_behind(value, axis, steps):
    count = lax.axis_size(axis)
    pairs = [(source, (source + steps) % count) for source in range(count)]
    return lax.ppermute(value, axis, pairs)


def shards(
    position,
    orient,
    velocity,
    history,
    template,
    cross_local,
    cross_ghost,
    cross_count,
    inner_first,
    inner_gap,
    mig_index,
    mig_dest,
):
    lists = [v.reshape(1, PAIRS) for v in (cross_local, cross_ghost, inner_first, inner_gap, mig_index, mig_dest)]
    loads = [
        pltpu.with_memory_space_constraint(v, pltpu.HBM)
        for v in (position, orient, history, velocity, template, *lists)
    ]
    packed, velocity, template, local, ghost, first, gap, leaving, dest = pl.pallas_call(
        pack_kernel,
        out_shape=(array(PACKED, CLUMPS), array(6, CLUMPS), array(3, MEMBERS)) + (array(1, PAIRS, dtype=I32),) * 6,
        in_specs=[hbm()] * 11 + [smem()],
        out_specs=(vmem(),) * 9,
        scratch_shapes=[
            pltpu.VMEM((3, CLUMPS), F32),
            pltpu.VMEM((4, CLUMPS), F32),
            pltpu.SemaphoreType.DMA((11,)),
        ],
        compiler_params=small(),
        name="pack",
    )(*loads, cross_count)
    slab_next = from_behind(packed, "slab", -1)
    slab_back = from_behind(packed, "slab", 1)
    brick_next = from_behind(packed, "brick", -1)
    totals, route, departed, spread, target = pl.pallas_call(
        inner_kernel,
        out_shape=(
            array(PACKED, CLUMPS),
            array(BRICKS * CHUNK, CLUMPS),
            array(8, CLUMPS),
            array(3, MEMBERS, LANES),
            array(7, HALF, LANES),
        ),
        in_specs=[vmem()] * 7,
        out_specs=(vmem(),) * 5,
        scratch_shapes=[pltpu.VMEM((4, MEMBERS, LANES), F32)],
        cost_estimate=cost(20_000_000),
        compiler_params=small(),
        name="inner",
    )(packed, template, first, gap, leaving, dest, local)
    totals, picked = pl.pallas_call(
        slab_kernel,
        out_shape=(array(PACKED, CLUMPS), array(PACKED, LANES)),
        in_specs=[vmem()] * 6,
        out_specs=(vmem(),) * 2,
        scratch_shapes=[pltpu.VMEM((4, MEMBERS, LANES), F32)],
        cost_estimate=cost(10_000_000),
        compiler_params=small(),
        name="slab",
    )(packed, slab_back, slab_next, totals, spread, ghost)
    state, back, buffer = pl.pallas_call(
        brick_kernel,
        out_shape=(array(LANES, CLUMPS), array(PACKED, CLUMPS), array(BRICKS * CHUNK, LANES)),
        in_specs=[vmem()] * 9 + [smem(), vmem()],
        out_specs=(vmem(),) * 3,
        scratch_shapes=[
            pltpu.VMEM((4, MEMBERS, LANES), F32),
            pltpu.VMEM((4, 8 * MEMBERS, LANES), F32),
        ],
        cost_estimate=cost(15_000_000),
        compiler_params=small(),
        name="brick",
    )(packed, brick_next, picked, totals, velocity, spread, target, local, ghost, cross_count, route)
    arrived = lax.all_to_all(buffer.reshape(BRICKS, CHUNK, LANES), "brick", split_axis=0, concat_axis=0)
    back = from_behind(back, "brick", 1)
    staying = pl.pallas_call(
        stay_kernel,
        out_shape=array(77, CLUMPS),
        in_specs=[vmem()] * 4,
        out_specs=vmem(),
        cost_estimate=cost(5_000_000),
        compiler_params=small(),
        name="stay",
    )(state, packed, back, departed)
    arrivals = pl.pallas_call(
        turn_kernel,
        out_shape=array(77, BRICKS * SLOT_CAP),
        in_specs=[vmem()],
        out_specs=vmem(),
        scratch_shapes=[pltpu.VMEM((BRICKS * SLOT_CAP, LANES), F32)],
        compiler_params=small(),
        name="turn",
    )(arrived.reshape(BRICKS * CHUNK, LANES))
    return (staying, arrivals)


def solution(mesh):
    both = ("slab", "brick")
    return jax.shard_map(
        shards,
        mesh=mesh,
        in_specs=(
            P(None, both),
            P(None, both),
            P(None, both),
            P(None, both),
            P(),
            P(both),
            P(both),
            P(both),
            P(both),
            P(both),
            P(both),
            P(both, None),
        ),
        out_specs=(P(None, both), P(None, both)),
        check_vma=False,
    )
```

```python
import jax
import jax.numpy as jnp
from jax import lax
from jax.experimental import pallas as pl
from jax.experimental.pallas import tpu as pltpu
from jax.sharding import PartitionSpec as P

MEMBERS = 64
CLUMPS = 256
LANES = 128
PAIRS = 64
HALF = MEMBERS // 2
SLOT_CAP = 2
BRICKS = 64
FIRST = 36
ORDER = [FIRST ^ k for k in range(BRICKS)]
VMEM_LIMIT = 8 * 1024 * 1024
IDLE = 1024

DIAMETER = 0.3
SOFTENING = 0.0001
TIME_STEP = 0.02
INERTIA_SCALE = 0.05
HISTORY_DECAY = 0.9

POS = MEMBERS
ORI = MEMBERS + 3
LISTS = MEMBERS + 7
PACKED = MEMBERS + 8

LAST = (((1,), (1,)), ((), ()))
F32 = jnp.float32
BF16 = jnp.bfloat16
I32 = jnp.int32


def parts_of(value):
    high = value.astype(BF16).astype(F32)
    rest = value - high
    middle = rest.astype(BF16).astype(F32)
    return jnp.concatenate([high, middle, rest - middle], 0).astype(BF16)


def sum_parts(value):
    rows = value.shape[0] // 3
    return value[:rows] + value[rows : 2 * rows] + value[2 * rows :]


def one_hot(index_row, rows=CLUMPS):
    count = lax.broadcasted_iota(I32, (rows, index_row.shape[1]), 0)
    return jnp.where(count == index_row, 1.0, 0.0).astype(F32).astype(BF16)


def gather(parts, chosen):
    return sum_parts(jnp.dot(parts, chosen, preferred_element_type=F32))


def scatter(value, chosen):
    return sum_parts(lax.dot_general(parts_of(value), chosen, LAST, preferred_element_type=F32))


def arms_of(picked, template):
    quat = [picked[ORI + k : ORI + k + 1] for k in range(4)]
    scale = lax.rsqrt(quat[0] * quat[0] + quat[1] * quat[1] + quat[2] * quat[2] + quat[3] * quat[3])
    qw, qx, qy, qz = [q * scale for q in quat]
    matrix = [
        [1.0 - 2.0 * (qy * qy + qz * qz), 2.0 * (qx * qy - qw * qz), 2.0 * (qx * qz + qw * qy)],
        [2.0 * (qx * qy + qw * qz), 1.0 - 2.0 * (qx * qx + qz * qz), 2.0 * (qy * qz - qw * qx)],
        [2.0 * (qx * qz - qw * qy), 2.0 * (qy * qz + qw * qx), 1.0 - 2.0 * (qx * qx + qy * qy)],
    ]
    return [row[0] * template[0] + row[1] * template[1] + row[2] * template[2] for row in matrix]


def spread_template(template_ref):
    padded = jnp.concatenate([template_ref[...], jnp.zeros((5, MEMBERS), F32)], 0)
    turned = padded.T
    return [jnp.broadcast_to(turned[:, k : k + 1], (MEMBERS, LANES)) for k in range(3)]


def twice(row):
    return jnp.concatenate([row, row], 1)


def halves(value):
    lane = lax.broadcasted_iota(I32, (HALF, LANES), 1)
    return jnp.where(lane < PAIRS, value[:HALF], value[HALF:])


def place_source(src_ref, picked, arm, shift):
    for k in range(3):
        src_ref[k] = (picked[POS + k : POS + k + 1] + shift[k]) + arm[k]
    src_ref[3] = 10.0 + 10.0 * picked[0:MEMBERS]


def contact(place, weight, src_ref):
    def step(b, sums):
        other = [src_ref[k, pl.ds(b, 1), :] for k in range(4)]
        dx = place[0] - other[0]
        dy = place[1] - other[1]
        dz = place[2] - other[2]
        square = dx * dx + dy * dy + (dz * dz + SOFTENING)
        inverse = lax.rsqrt(square)
        margin = jnp.maximum(DIAMETER - square * inverse, 0.0)
        push = margin * inverse * (weight + other[3])
        return (sums[0] + push * dx, sums[1] + push * dy, sums[2] + push * dz, sums[3] + margin)

    zero = jnp.zeros((HALF, LANES), F32)
    return lax.fori_loop(0, MEMBERS, step, (zero, zero, zero, zero), unroll=4)


def body_rows(arm, force):
    turn = [
        arm[1] * force[2] - arm[2] * force[1],
        arm[2] * force[0] - arm[0] * force[2],
        arm[0] * force[1] - arm[1] * force[0],
    ]
    return jnp.concatenate(
        [jnp.sum(v, axis=0, keepdims=True) for v in list(force) + turn]
        + [jnp.zeros((2, LANES), F32)],
        0,
    )


def full_batch(picked, template, src_ref):
    arm = arms_of(picked, template)
    weight = 10.0 + 10.0 * picked[0:MEMBERS]
    tail = jnp.zeros((8, LANES), F32)
    margins = []
    for cut in (slice(0, HALF), slice(HALF, MEMBERS)):
        own = [a[cut] for a in arm]
        place = [picked[POS + k : POS + k + 1] + own[k] for k in range(3)]
        out = contact(place, weight[cut], src_ref)
        margins.append(out[3])
        tail = tail + body_rows(own, out[0:3])
    return jnp.concatenate(margins + [tail], 0)


def half_targets(picked, template):
    arm = arms_of(picked, [halves(t) for t in template])
    weight = 10.0 + 10.0 * halves(picked[0:MEMBERS])
    place = [picked[POS + k : POS + k + 1] + arm[k] for k in range(3)]
    return place, weight, arm


def half_rows(arm, out):
    lane = lax.broadcasted_iota(I32, (HALF, LANES), 1)
    lower = jnp.where(lane < PAIRS, out[3], 0.0)
    upper = jnp.where(lane < PAIRS, 0.0, out[3])
    return jnp.concatenate([lower, upper, body_rows(arm, out[0:3])], 0)


def contact_both(place, weight, src_ref, acc_ref):
    def step(b, sums):
        other = [src_ref[k, pl.ds(b, 1), :] for k in range(4)]
        offset = [place[k] - other[k] for k in range(3)]
        square = offset[0] * offset[0] + offset[1] * offset[1] + (offset[2] * offset[2] + SOFTENING)
        inverse = lax.rsqrt(square)
        margin = jnp.maximum(DIAMETER - square * inverse, 0.0)
        push = margin * inverse * (weight + other[3])
        terms = [push * d for d in offset] + [margin]
        for k in range(4):
            acc_ref[k, pl.ds(pl.multiple_of(b * 8, 8), 8), :] = jnp.sum(terms[k].reshape(HALF // 8, 8, LANES), axis=0)
        return tuple(total + term for total, term in zip(sums, terms))

    zero = jnp.zeros((HALF, LANES), F32)
    return lax.fori_loop(0, MEMBERS, step, (zero, zero, zero, zero), unroll=4)


def source_sums(acc_ref):
    out = []
    for k in range(4):
        rows = [acc_ref[k, pl.ds(r, MEMBERS, stride=8), :] for r in range(8)]
        out.append(((rows[0] + rows[1]) + (rows[2] + rows[3])) + ((rows[4] + rows[5]) + (rows[6] + rows[7])))
    return out


def place_of(brick):
    return jnp.bitwise_xor(brick, FIRST)


def in_order(rows):
    blocks = [rows[8 * k : 8 * k + 8] for k in range(BRICKS // 4)]
    return jnp.concatenate([blocks[(FIRST // 4) ^ k] for k in range(BRICKS // 4)], 0)


def routes(leaving, dest):
    to = one_hot(dest, BRICKS)
    before = lax.broadcasted_iota(I32, (PAIRS, PAIRS), 0) < lax.broadcasted_iota(I32, (PAIRS, PAIRS), 1)
    before = jnp.where(before, 1.0, 0.0).astype(BF16)
    earlier = jnp.dot(to, before, preferred_element_type=F32)
    rank = jnp.sum(earlier * to.astype(F32), axis=0, keepdims=True).astype(I32)
    column = one_hot(place_of(dest) * SLOT_CAP + rank, BRICKS * SLOT_CAP)
    leaves = one_hot(leaving)
    ones = jnp.ones((8, PAIRS), F32).astype(BF16)
    return (
        lax.dot_general(column, leaves, LAST, preferred_element_type=F32),
        lax.dot_general(ones, leaves, LAST, preferred_element_type=F32),
    )


def pack_kernel(
    pos_hbm,
    ori_hbm,
    hist_hbm,
    velocity_hbm,
    template_hbm,
    local_hbm,
    ghost_hbm,
    first_hbm,
    gap_hbm,
    leaving_hbm,
    dest_hbm,
    count_ref,
    packed_ref,
    velocity_ref,
    template_ref,
    local_ref,
    ghost_ref,
    first_ref,
    gap_ref,
    leaving_ref,
    dest_ref,
    pos_ref,
    ori_ref,
    sems,
):
    moves = [
        (hist_hbm, packed_ref.at[0:MEMBERS]),
        (pos_hbm, pos_ref),
        (ori_hbm, ori_ref),
        (local_hbm, local_ref),
        (ghost_hbm, ghost_ref),
        (leaving_hbm, leaving_ref),
        (dest_hbm, dest_ref),
        (velocity_hbm, velocity_ref),
        (template_hbm, template_ref),
        (first_hbm, first_ref),
        (gap_hbm, gap_ref),
    ]
    copies = [pltpu.make_async_copy(a, b, sems.at[k]) for k, (a, b) in enumerate(moves)]
    for copy in copies:
        copy.start()
    for copy in copies[1:]:
        copy.wait()
    live = lax.broadcasted_iota(I32, (1, PAIRS), 1) < count_ref[0]
    ghost = ghost_ref[...]
    code = jnp.where(live, ghost, ghost + IDLE)
    lists = jnp.concatenate([local_ref[...], local_ref[...], code, code], 1).astype(F32)
    packed_ref[MEMBERS:PACKED] = jnp.concatenate([pos_ref[...], ori_ref[...], lists], 0)
    copies[0].wait()


def inner_kernel(
    packed_ref,
    template_ref,
    first_ref,
    gap_ref,
    leaving_ref,
    dest_ref,
    totals_ref,
    route_ref,
    departed_ref,
    spread_ref,
    src_ref,
    acc_ref,
):
    template = spread_template(template_ref)
    for k in range(3):
        spread_ref[k] = template[k]
    route_ref[...], departed_ref[...] = routes(leaving_ref[...], dest_ref[...])

    own = parts_of(packed_ref[...])
    first = first_ref[...]
    second = one_hot(twice(jnp.bitwise_and(first + gap_ref[...], CLUMPS - 1)))
    first = one_hot(twice(first))
    picked = gather(own, second)
    arm_b = arms_of(picked, template)
    place_source(src_ref, picked, arm_b, (0.0, 0.0, 0.0))
    place, weight, arm = half_targets(gather(own, first), template)
    rows = half_rows(arm, contact_both(place, weight, src_ref, acc_ref))
    force_x, force_y, force_z, margin = source_sums(acc_ref)
    other = jnp.concatenate([margin, -body_rows(arm_b, (force_x, force_y, force_z))], 0)
    totals_ref[...] = scatter(rows, first) + scatter(other, second)


def outer_kernel(
    packed_ref,
    totals_ref,
    velocity_ref,
    spread_ref,
    local_ref,
    ghost_ref,
    count_ref,
    route_ref,
    slab_next_ref,
    brick_next_ref,
    brick_back_ref,
    slab_back_ref,
    state_ref,
    buffer_ref,
    src_ref,
    src2_ref,
):
    template = [spread_ref[k] for k in range(3)]
    lane = lax.broadcasted_iota(I32, (1, LANES), 1)
    low = lane < PAIRS
    live = lax.broadcasted_iota(I32, (1, PAIRS), 1) < count_ref[0]
    local_code = twice(jnp.where(live, local_ref[...], IDLE))
    local = twice(local_ref[...])
    ghost = twice(ghost_ref[...])
    brick_lists = brick_back_ref[LISTS : LISTS + 1].astype(I32)
    slab_lists = slab_back_ref[LISTS : LISTS + 1].astype(I32)
    brick_local, brick_code = brick_lists[:, :LANES], brick_lists[:, LANES:]
    slab_local, slab_code = slab_lists[:, :LANES], slab_lists[:, LANES:]

    own = parts_of(packed_ref[...])
    source = (
        gather(parts_of(brick_next_ref[...]), one_hot(jnp.where(low, ghost, -1)))
        + gather(parts_of(slab_next_ref[...]), one_hot(jnp.where(low, ghost - CLUMPS, -1)))
        + gather(parts_of(brick_back_ref[...]), one_hot(jnp.where(low, -1, brick_local)))
    )
    near = ghost < CLUMPS
    shift = (
        jnp.where(low, jnp.where(near, 0.0, 1.0), 0.0),
        jnp.where(low, jnp.where(near, 1.0, 0.0), -1.0),
        0.0,
    )
    place_source(src_ref, source, arms_of(source, template), shift)
    picked = gather(own, one_hot(jnp.where(low, local, jnp.bitwise_and(brick_code, CLUMPS - 1))))
    source = gather(parts_of(slab_back_ref[...]), one_hot(slab_local))
    place_source(src2_ref, source, arms_of(source, template), (-1.0, 0.0, 0.0))
    chosen = one_hot(jnp.bitwise_and(slab_code, CLUMPS - 1))
    place, weight, arm = half_targets(gather(own, chosen), template)

    rows2 = half_rows(arm, contact(place, weight, src2_ref))
    rows = full_batch(picked, template, src_ref)
    totals = (
        totals_ref[...]
        + scatter(rows2, one_hot(slab_code - CLUMPS))
        + scatter(rows, one_hot(jnp.where(low, local_code, brick_code)))
    )

    state = packed_ref[...]
    velocity = velocity_ref[...]
    ow, ox, oy, oz = orient = [state[ORI + k : ORI + k + 1] for k in range(4)]
    linear = velocity[0:3] + TIME_STEP * totals[MEMBERS : MEMBERS + 3]
    angular = velocity[3:6] + TIME_STEP * totals[MEMBERS + 3 : MEMBERS + 6] / INERTIA_SCALE
    centre = state[POS : POS + 3] + TIME_STEP * linear
    wx, wy, wz = [angular[k : k + 1] for k in range(3)]
    spin = [
        -(wx * ox + wy * oy + wz * oz),
        ow * wx + (wy * oz - wz * oy),
        ow * wy + (wz * ox - wx * oz),
        ow * wz + (wx * oy - wy * ox),
    ]
    turned = [orient[k] + 0.5 * TIME_STEP * spin[k] for k in range(4)]
    history = HISTORY_DECAY * state[0:MEMBERS] + totals[0:MEMBERS]
    full = jnp.concatenate(
        [history, centre] + turned + [linear, angular, jnp.zeros((LANES - 77, CLUMPS), F32)], 0
    )
    state_ref[...] = full
    slots = lax.dot_general(route_ref[...].astype(BF16), parts_of(full), LAST, preferred_element_type=F32)
    buffer_ref[...] = slots[:, :LANES] + slots[:, LANES : 2 * LANES] + slots[:, 2 * LANES :]


def stay_kernel(state_ref, departed_ref, staying_ref):
    departed = departed_ref[0:1] > 0.5
    staying_ref[0:13] = jnp.where(departed, 0.0, state_ref[MEMBERS : MEMBERS + 13])
    staying_ref[13:77] = jnp.where(departed, 0.0, state_ref[0:MEMBERS])


def turn_kernel(in_ref, out_ref):
    turned = in_order(in_ref[...]).T
    out_ref[0:13] = turned[MEMBERS : MEMBERS + 13]
    out_ref[13:77] = turned[0:MEMBERS]


def vmem():
    return pl.BlockSpec(memory_space=pltpu.VMEM)


def smem():
    return pl.BlockSpec(memory_space=pltpu.SMEM)


def hbm():
    return pl.BlockSpec(memory_space=pltpu.HBM)


def small():
    return pltpu.CompilerParams(vmem_limit_bytes=VMEM_LIMIT)


def cost(flops):
    return pl.CostEstimate(flops=flops, bytes_accessed=400_000, transcendentals=flops // 30)


def array(*shape, dtype=F32):
    return jax.ShapeDtypeStruct(shape, dtype)


def from_behind(value, axis, steps):
    count = lax.axis_size(axis)
    pairs = [(source, (source + steps) % count) for source in range(count)]
    return lax.ppermute(value, axis, pairs)


def shards(
    position,
    orient,
    velocity,
    history,
    template,
    cross_local,
    cross_ghost,
    cross_count,
    inner_first,
    inner_gap,
    mig_index,
    mig_dest,
):
    lists = [v.reshape(1, PAIRS) for v in (cross_local, cross_ghost, inner_first, inner_gap, mig_index, mig_dest)]
    loads = [
        pltpu.with_memory_space_constraint(v, pltpu.HBM)
        for v in (position, orient, history, velocity, template, *lists)
    ]
    packed, velocity, template, local, ghost, first, gap, leaving, dest = pl.pallas_call(
        pack_kernel,
        out_shape=(array(PACKED, CLUMPS), array(6, CLUMPS), array(3, MEMBERS)) + (array(1, PAIRS, dtype=I32),) * 6,
        in_specs=[hbm()] * 11 + [smem()],
        out_specs=(vmem(),) * 9,
        scratch_shapes=[
            pltpu.VMEM((3, CLUMPS), F32),
            pltpu.VMEM((4, CLUMPS), F32),
            pltpu.SemaphoreType.DMA((11,)),
        ],
        compiler_params=small(),
        name="pack",
    )(*loads, cross_count)
    slab_next = from_behind(packed, "slab", -1)
    slab_back = from_behind(packed, "slab", 1)
    brick_next = from_behind(packed, "brick", -1)
    brick_back = from_behind(packed, "brick", 1)
    totals, route, departed, spread = pl.pallas_call(
        inner_kernel,
        out_shape=(
            array(PACKED, CLUMPS),
            array(BRICKS * SLOT_CAP, CLUMPS),
            array(8, CLUMPS),
            array(3, MEMBERS, LANES),
        ),
        in_specs=[vmem()] * 6,
        out_specs=(vmem(),) * 4,
        scratch_shapes=[
            pltpu.VMEM((4, MEMBERS, LANES), F32),
            pltpu.VMEM((4, 8 * MEMBERS, LANES), F32),
        ],
        cost_estimate=cost(20_000_000),
        compiler_params=small(),
        name="inner",
    )(packed, template, first, gap, leaving, dest)
    state, buffer = pl.pallas_call(
        outer_kernel,
        out_shape=(array(LANES, CLUMPS), array(BRICKS * SLOT_CAP, LANES)),
        in_specs=[vmem()] * 6 + [smem()] + [vmem()] * 5,
        out_specs=(vmem(),) * 2,
        scratch_shapes=[pltpu.VMEM((4, MEMBERS, LANES), F32)] * 2,
        cost_estimate=cost(25_000_000),
        compiler_params=small(),
        name="outer",
    )(
        packed,
        totals,
        velocity,
        spread,
        local,
        ghost,
        cross_count,
        route,
        slab_next,
        brick_next,
        brick_back,
        slab_back,
    )
    arrived = lax.all_to_all(
        buffer.reshape(BRICKS, SLOT_CAP, LANES),
        "brick",
        split_axis=0,
        concat_axis=0,
        axis_index_groups=[ORDER],
    )
    staying = pl.pallas_call(
        stay_kernel,
        out_shape=array(77, CLUMPS),
        in_specs=[vmem()] * 2,
        out_specs=vmem(),
        cost_estimate=cost(5_000_000),
        compiler_params=small(),
        name="stay",
    )(state, departed)
    arrivals = pl.pallas_call(
        turn_kernel,
        out_shape=array(77, BRICKS * SLOT_CAP),
        in_specs=[vmem()],
        out_specs=vmem(),
        compiler_params=small(),
        name="turn",
    )(arrived.reshape(BRICKS * SLOT_CAP, LANES))
    return (staying, arrivals)


def solution(mesh):
    both = ("slab", "brick")
    return jax.shard_map(
        shards,
        mesh=mesh,
        in_specs=(
            P(None, both),
            P(None, both),
            P(None, both),
            P(None, both),
            P(),
            P(both),
            P(both),
            P(both),
            P(both),
            P(both),
            P(both),
            P(both, None),
        ),
        out_specs=(P(None, both), P(None, both)),
        check_vma=False,
    )
```

```python
import jax
import jax.numpy as jnp
from jax import lax
from jax.experimental import pallas as pl
from jax.experimental.pallas import tpu as pltpu
from jax.sharding import PartitionSpec as P

MEMBERS = 64
CLUMPS = 256
LANES = 128
PAIRS = 64
HALF = MEMBERS // 2
SLOT_CAP = 2
BRICKS = 64
FIRST = 52
ORDER = [FIRST ^ k for k in range(BRICKS)]
VMEM_LIMIT = 8 * 1024 * 1024
IDLE = 1024

DIAMETER = 0.3
SOFTENING = 0.0001
TIME_STEP = 0.02
INERTIA_SCALE = 0.05
HISTORY_DECAY = 0.9

POS = MEMBERS
ORI = MEMBERS + 3
LISTS = MEMBERS + 7
PACKED = MEMBERS + 8

LAST = (((1,), (1,)), ((), ()))
F32 = jnp.float32
BF16 = jnp.bfloat16
I32 = jnp.int32


def parts_of(value):
    high = value.astype(BF16).astype(F32)
    rest = value - high
    middle = rest.astype(BF16).astype(F32)
    return jnp.concatenate([high, middle, rest - middle], 0).astype(BF16)


def sum_parts(value):
    rows = value.shape[0] // 3
    return value[:rows] + value[rows : 2 * rows] + value[2 * rows :]


def one_hot(index_row, rows=CLUMPS):
    count = lax.broadcasted_iota(I32, (rows, index_row.shape[1]), 0)
    return jnp.where(count == index_row, 1.0, 0.0).astype(F32).astype(BF16)


def gather(parts, chosen):
    return sum_parts(jnp.dot(parts, chosen, preferred_element_type=F32))


def scatter(value, chosen):
    return sum_parts(lax.dot_general(parts_of(value), chosen, LAST, preferred_element_type=F32))


def arms_of(picked, template):
    quat = [picked[ORI + k : ORI + k + 1] for k in range(4)]
    scale = lax.rsqrt(quat[0] * quat[0] + quat[1] * quat[1] + quat[2] * quat[2] + quat[3] * quat[3])
    qw, qx, qy, qz = [q * scale for q in quat]
    matrix = [
        [1.0 - 2.0 * (qy * qy + qz * qz), 2.0 * (qx * qy - qw * qz), 2.0 * (qx * qz + qw * qy)],
        [2.0 * (qx * qy + qw * qz), 1.0 - 2.0 * (qx * qx + qz * qz), 2.0 * (qy * qz - qw * qx)],
        [2.0 * (qx * qz - qw * qy), 2.0 * (qy * qz + qw * qx), 1.0 - 2.0 * (qx * qx + qy * qy)],
    ]
    return [row[0] * template[0] + row[1] * template[1] + row[2] * template[2] for row in matrix]


def spread_template(template_ref):
    padded = jnp.concatenate([template_ref[...], jnp.zeros((5, MEMBERS), F32)], 0)
    turned = padded.T
    return [jnp.broadcast_to(turned[:, k : k + 1], (MEMBERS, LANES)) for k in range(3)]


def twice(row):
    return jnp.concatenate([row, row], 1)


def halves(value):
    lane = lax.broadcasted_iota(I32, (HALF, LANES), 1)
    return jnp.where(lane < PAIRS, value[:HALF], value[HALF:])


def place_source(src_ref, picked, arm, shift):
    for k in range(3):
        src_ref[k] = (picked[POS + k : POS + k + 1] + shift[k]) + arm[k]
    src_ref[3] = 10.0 + 10.0 * picked[0:MEMBERS]


def contact(place, weight, src_ref):
    def step(b, sums):
        other = [src_ref[k, pl.ds(b, 1), :] for k in range(4)]
        dx = place[0] - other[0]
        dy = place[1] - other[1]
        dz = place[2] - other[2]
        square = dx * dx + dy * dy + (dz * dz + SOFTENING)
        inverse = lax.rsqrt(square)
        margin = jnp.maximum(DIAMETER - square * inverse, 0.0)
        push = margin * inverse * (weight + other[3])
        return (sums[0] + push * dx, sums[1] + push * dy, sums[2] + push * dz, sums[3] + margin)

    zero = jnp.zeros((HALF, LANES), F32)
    return lax.fori_loop(0, MEMBERS, step, (zero, zero, zero, zero), unroll=4)


def body_rows(arm, force):
    turn = [
        arm[1] * force[2] - arm[2] * force[1],
        arm[2] * force[0] - arm[0] * force[2],
        arm[0] * force[1] - arm[1] * force[0],
    ]
    return jnp.concatenate(
        [jnp.sum(v, axis=0, keepdims=True) for v in list(force) + turn]
        + [jnp.zeros((2, LANES), F32)],
        0,
    )


def full_batch(picked, template, src_ref):
    arm = arms_of(picked, template)
    weight = 10.0 + 10.0 * picked[0:MEMBERS]
    tail = jnp.zeros((8, LANES), F32)
    margins = []
    for cut in (slice(0, HALF), slice(HALF, MEMBERS)):
        own = [a[cut] for a in arm]
        place = [picked[POS + k : POS + k + 1] + own[k] for k in range(3)]
        out = contact(place, weight[cut], src_ref)
        margins.append(out[3])
        tail = tail + body_rows(own, out[0:3])
    return jnp.concatenate(margins + [tail], 0)


def half_targets(picked, template):
    arm = arms_of(picked, [halves(t) for t in template])
    weight = 10.0 + 10.0 * halves(picked[0:MEMBERS])
    place = [picked[POS + k : POS + k + 1] + arm[k] for k in range(3)]
    return place, weight, arm


def half_rows(arm, out):
    lane = lax.broadcasted_iota(I32, (HALF, LANES), 1)
    lower = jnp.where(lane < PAIRS, out[3], 0.0)
    upper = jnp.where(lane < PAIRS, 0.0, out[3])
    return jnp.concatenate([lower, upper, body_rows(arm, out[0:3])], 0)


def contact_both(place, weight, src_ref, acc_ref):
    def step(b, sums):
        other = [src_ref[k, pl.ds(b, 1), :] for k in range(4)]
        offset = [place[k] - other[k] for k in range(3)]
        square = offset[0] * offset[0] + offset[1] * offset[1] + (offset[2] * offset[2] + SOFTENING)
        inverse = lax.rsqrt(square)
        margin = jnp.maximum(DIAMETER - square * inverse, 0.0)
        push = margin * inverse * (weight + other[3])
        terms = [push * d for d in offset] + [margin]
        for k in range(4):
            acc_ref[k, pl.ds(pl.multiple_of(b * 8, 8), 8), :] = jnp.sum(terms[k].reshape(HALF // 8, 8, LANES), axis=0)
        return tuple(total + term for total, term in zip(sums, terms))

    zero = jnp.zeros((HALF, LANES), F32)
    return lax.fori_loop(0, MEMBERS, step, (zero, zero, zero, zero), unroll=4)


def source_sums(acc_ref):
    out = []
    for k in range(4):
        rows = [acc_ref[k, pl.ds(r, MEMBERS, stride=8), :] for r in range(8)]
        out.append(((rows[0] + rows[1]) + (rows[2] + rows[3])) + ((rows[4] + rows[5]) + (rows[6] + rows[7])))
    return out


def place_of(brick):
    return jnp.bitwise_xor(brick, FIRST)


def in_order(rows):
    blocks = [rows[8 * k : 8 * k + 8] for k in range(BRICKS // 4)]
    return jnp.concatenate([blocks[(FIRST // 4) ^ k] for k in range(BRICKS // 4)], 0)


def routes(leaving, dest):
    to = one_hot(dest, BRICKS)
    before = lax.broadcasted_iota(I32, (PAIRS, PAIRS), 0) < lax.broadcasted_iota(I32, (PAIRS, PAIRS), 1)
    before = jnp.where(before, 1.0, 0.0).astype(BF16)
    earlier = jnp.dot(to, before, preferred_element_type=F32)
    rank = jnp.sum(earlier * to.astype(F32), axis=0, keepdims=True).astype(I32)
    column = one_hot(place_of(dest) * SLOT_CAP + rank, BRICKS * SLOT_CAP)
    leaves = one_hot(leaving)
    ones = jnp.ones((8, PAIRS), F32).astype(BF16)
    return (
        lax.dot_general(column, leaves, LAST, preferred_element_type=F32),
        lax.dot_general(ones, leaves, LAST, preferred_element_type=F32),
    )


def pack_kernel(
    pos_hbm,
    ori_hbm,
    hist_hbm,
    velocity_hbm,
    template_hbm,
    local_hbm,
    ghost_hbm,
    first_hbm,
    gap_hbm,
    leaving_hbm,
    dest_hbm,
    count_ref,
    packed_ref,
    velocity_ref,
    template_ref,
    local_ref,
    ghost_ref,
    first_ref,
    gap_ref,
    leaving_ref,
    dest_ref,
    pos_ref,
    ori_ref,
    sems,
):
    moves = [
        (hist_hbm, packed_ref.at[0:MEMBERS]),
        (pos_hbm, pos_ref),
        (ori_hbm, ori_ref),
        (local_hbm, local_ref),
        (ghost_hbm, ghost_ref),
        (leaving_hbm, leaving_ref),
        (dest_hbm, dest_ref),
        (velocity_hbm, velocity_ref),
        (template_hbm, template_ref),
        (first_hbm, first_ref),
        (gap_hbm, gap_ref),
    ]
    copies = [pltpu.make_async_copy(a, b, sems.at[k]) for k, (a, b) in enumerate(moves)]
    for copy in copies:
        copy.start()
    for copy in copies[1:]:
        copy.wait()
    live = lax.broadcasted_iota(I32, (1, PAIRS), 1) < count_ref[0]
    ghost = ghost_ref[...]
    code = jnp.where(live, ghost, ghost + IDLE)
    lists = jnp.concatenate([local_ref[...], local_ref[...], code, code], 1).astype(F32)
    packed_ref[MEMBERS:PACKED] = jnp.concatenate([pos_ref[...], ori_ref[...], lists], 0)
    copies[0].wait()


def inner_kernel(
    packed_ref,
    template_ref,
    first_ref,
    gap_ref,
    leaving_ref,
    dest_ref,
    local_ref,
    totals_ref,
    route_ref,
    departed_ref,
    spread_ref,
    target_ref,
    src_ref,
    acc_ref,
):
    template = spread_template(template_ref)
    for k in range(3):
        spread_ref[k] = template[k]
    route_ref[...], departed_ref[...] = routes(leaving_ref[...], dest_ref[...])

    own = parts_of(packed_ref[...])
    place, weight, arm = half_targets(gather(own, one_hot(twice(local_ref[...]))), template)
    for k in range(3):
        target_ref[k] = place[k]
        target_ref[4 + k] = arm[k]
    target_ref[3] = weight

    first = first_ref[...]
    second = one_hot(twice(jnp.bitwise_and(first + gap_ref[...], CLUMPS - 1)))
    first = one_hot(twice(first))
    picked = gather(own, second)
    arm_b = arms_of(picked, template)
    place_source(src_ref, picked, arm_b, (0.0, 0.0, 0.0))
    place, weight, arm = half_targets(gather(own, first), template)
    rows = half_rows(arm, contact_both(place, weight, src_ref, acc_ref))
    force_x, force_y, force_z, margin = source_sums(acc_ref)
    other = jnp.concatenate([margin, -body_rows(arm_b, (force_x, force_y, force_z))], 0)
    totals_ref[...] = scatter(rows, first) + scatter(other, second)


def before_kernel(packed_ref, inner_ref, spread_ref, brick_back_ref, slab_back_ref, totals_ref, src_ref):
    template = [spread_ref[k] for k in range(3)]
    low = lax.broadcasted_iota(I32, (1, LANES), 1) < PAIRS
    brick_lists = brick_back_ref[LISTS : LISTS + 1].astype(I32)
    slab_lists = slab_back_ref[LISTS : LISTS + 1].astype(I32)
    brick_local, brick_code = brick_lists[:, :LANES], brick_lists[:, LANES:]
    slab_local, slab_code = slab_lists[:, :LANES], slab_lists[:, LANES:]
    source = gather(parts_of(brick_back_ref[...]), one_hot(jnp.where(low, brick_local, -1))) + gather(
        parts_of(slab_back_ref[...]), one_hot(jnp.where(low, -1, slab_local))
    )
    shift = (jnp.where(low, 0.0, -1.0), jnp.where(low, -1.0, 0.0), 0.0)
    place_source(src_ref, source, arms_of(source, template), shift)
    chosen = one_hot(jnp.bitwise_and(jnp.where(low, brick_code, slab_code), CLUMPS - 1))
    rows = full_batch(gather(parts_of(packed_ref[...]), chosen), template, src_ref)
    totals_ref[...] = inner_ref[...] + scatter(rows, one_hot(jnp.where(low, brick_code, slab_code - CLUMPS)))


def outer_kernel(
    packed_ref,
    totals_ref,
    velocity_ref,
    spread_ref,
    target_ref,
    local_ref,
    ghost_ref,
    count_ref,
    route_ref,
    brick_next_ref,
    slab_next_ref,
    state_ref,
    buffer_ref,
    src_ref,
):
    template = [spread_ref[k] for k in range(3)]
    live = lax.broadcasted_iota(I32, (1, PAIRS), 1) < count_ref[0]
    local = twice(jnp.where(live, local_ref[...], IDLE))
    ghost = twice(ghost_ref[...])
    near = ghost < CLUMPS
    source = gather(parts_of(brick_next_ref[...]), one_hot(ghost)) + gather(
        parts_of(slab_next_ref[...]), one_hot(ghost - CLUMPS)
    )
    shift = (jnp.where(near, 0.0, 1.0), jnp.where(near, 1.0, 0.0), 0.0)
    place_source(src_ref, source, arms_of(source, template), shift)
    out = contact([target_ref[k] for k in range(3)], target_ref[3], src_ref)
    rows = half_rows([target_ref[4 + k] for k in range(3)], out)
    totals = totals_ref[...] + scatter(rows, one_hot(local))

    state = packed_ref[...]
    velocity = velocity_ref[...]
    ow, ox, oy, oz = orient = [state[ORI + k : ORI + k + 1] for k in range(4)]
    linear = velocity[0:3] + TIME_STEP * totals[MEMBERS : MEMBERS + 3]
    angular = velocity[3:6] + TIME_STEP * totals[MEMBERS + 3 : MEMBERS + 6] / INERTIA_SCALE
    centre = state[POS : POS + 3] + TIME_STEP * linear
    wx, wy, wz = [angular[k : k + 1] for k in range(3)]
    spin = [
        -(wx * ox + wy * oy + wz * oz),
        ow * wx + (wy * oz - wz * oy),
        ow * wy + (wz * ox - wx * oz),
        ow * wz + (wx * oy - wy * ox),
    ]
    turned = [orient[k] + 0.5 * TIME_STEP * spin[k] for k in range(4)]
    history = HISTORY_DECAY * state[0:MEMBERS] + totals[0:MEMBERS]
    full = jnp.concatenate(
        [history, centre] + turned + [linear, angular, jnp.zeros((LANES - 77, CLUMPS), F32)], 0
    )
    state_ref[...] = full
    slots = lax.dot_general(route_ref[...].astype(BF16), parts_of(full), LAST, preferred_element_type=F32)
    buffer_ref[...] = slots[:, :LANES] + slots[:, LANES : 2 * LANES] + slots[:, 2 * LANES :]


def finish_kernel(arrived_ref, state_ref, departed_ref, staying_ref, arrivals_ref):
    departed = departed_ref[0:1] > 0.5
    staying_ref[0:13] = jnp.where(departed, 0.0, state_ref[MEMBERS : MEMBERS + 13])
    staying_ref[13:77] = jnp.where(departed, 0.0, state_ref[0:MEMBERS])
    turned = in_order(arrived_ref[...]).T
    arrivals_ref[0:13] = turned[MEMBERS : MEMBERS + 13]
    arrivals_ref[13:77] = turned[0:MEMBERS]


def vmem():
    return pl.BlockSpec(memory_space=pltpu.VMEM)


def smem():
    return pl.BlockSpec(memory_space=pltpu.SMEM)


def hbm():
    return pl.BlockSpec(memory_space=pltpu.HBM)


def small():
    return pltpu.CompilerParams(vmem_limit_bytes=VMEM_LIMIT)


def cost(flops):
    return pl.CostEstimate(flops=flops, bytes_accessed=400_000, transcendentals=flops // 30)


def array(*shape, dtype=F32):
    return jax.ShapeDtypeStruct(shape, dtype)


def from_behind(value, axis, steps):
    count = lax.axis_size(axis)
    pairs = [(source, (source + steps) % count) for source in range(count)]
    return lax.ppermute(value, axis, pairs)


def shards(
    position,
    orient,
    velocity,
    history,
    template,
    cross_local,
    cross_ghost,
    cross_count,
    inner_first,
    inner_gap,
    mig_index,
    mig_dest,
):
    lists = [v.reshape(1, PAIRS) for v in (cross_local, cross_ghost, inner_first, inner_gap, mig_index, mig_dest)]
    loads = [
        pltpu.with_memory_space_constraint(v, pltpu.HBM)
        for v in (position, orient, history, velocity, template, *lists)
    ]
    packed, velocity, template, local, ghost, first, gap, leaving, dest = pl.pallas_call(
        pack_kernel,
        out_shape=(array(PACKED, CLUMPS), array(6, CLUMPS), array(3, MEMBERS)) + (array(1, PAIRS, dtype=I32),) * 6,
        in_specs=[hbm()] * 11 + [smem()],
        out_specs=(vmem(),) * 9,
        scratch_shapes=[
            pltpu.VMEM((3, CLUMPS), F32),
            pltpu.VMEM((4, CLUMPS), F32),
            pltpu.SemaphoreType.DMA((11,)),
        ],
        compiler_params=small(),
        name="pack",
    )(*loads, cross_count)
    slab_next = from_behind(packed, "slab", -1)
    slab_back = from_behind(packed, "slab", 1)
    brick_next = from_behind(packed, "brick", -1)
    brick_back = from_behind(packed, "brick", 1)
    totals, route, departed, spread, target = pl.pallas_call(
        inner_kernel,
        out_shape=(
            array(PACKED, CLUMPS),
            array(BRICKS * SLOT_CAP, CLUMPS),
            array(8, CLUMPS),
            array(3, MEMBERS, LANES),
            array(7, HALF, LANES),
        ),
        in_specs=[vmem()] * 7,
        out_specs=(vmem(),) * 5,
        scratch_shapes=[
            pltpu.VMEM((4, MEMBERS, LANES), F32),
            pltpu.VMEM((4, 8 * MEMBERS, LANES), F32),
        ],
        cost_estimate=cost(20_000_000),
        compiler_params=small(),
        name="inner",
    )(packed, template, first, gap, leaving, dest, local)
    totals = pl.pallas_call(
        before_kernel,
        out_shape=array(PACKED, CLUMPS),
        in_specs=[vmem()] * 5,
        out_specs=vmem(),
        scratch_shapes=[pltpu.VMEM((4, MEMBERS, LANES), F32)],
        cost_estimate=cost(20_000_000),
        compiler_params=small(),
        name="before",
    )(packed, totals, spread, brick_back, slab_back)
    state, buffer = pl.pallas_call(
        outer_kernel,
        out_shape=(array(LANES, CLUMPS), array(BRICKS * SLOT_CAP, LANES)),
        in_specs=[vmem()] * 7 + [smem()] + [vmem()] * 3,
        out_specs=(vmem(),) * 2,
        scratch_shapes=[pltpu.VMEM((4, MEMBERS, LANES), F32)],
        cost_estimate=cost(15_000_000),
        compiler_params=small(),
        name="outer",
    )(
        packed,
        totals,
        velocity,
        spread,
        target,
        local,
        ghost,
        cross_count,
        route,
        brick_next,
        slab_next,
    )
    arrived = lax.all_to_all(
        buffer.reshape(BRICKS, SLOT_CAP, LANES),
        "brick",
        split_axis=0,
        concat_axis=0,
        axis_index_groups=[ORDER],
    )
    staying, arrivals = pl.pallas_call(
        finish_kernel,
        out_shape=(array(77, CLUMPS), array(77, BRICKS * SLOT_CAP)),
        in_specs=[vmem()] * 3,
        out_specs=(vmem(),) * 2,
        cost_estimate=cost(5_000_000),
        compiler_params=small(),
        name="finish",
    )(arrived.reshape(BRICKS * SLOT_CAP, LANES), state, departed)
    return (staying, arrivals)


def solution(mesh):
    both = ("slab", "brick")
    return jax.shard_map(
        shards,
        mesh=mesh,
        in_specs=(
            P(None, both),
            P(None, both),
            P(None, both),
            P(None, both),
            P(),
            P(both),
            P(both),
            P(both),
            P(both),
            P(both),
            P(both),
            P(both, None),
        ),
        out_specs=(P(None, both), P(None, both)),
        check_vma=False,
    )
```

```python
import jax
import jax.numpy as jnp
from jax import lax
from jax.experimental import pallas as pl
from jax.experimental.pallas import tpu as pltpu
from jax.sharding import PartitionSpec as P

MEMBERS = 64
CLUMPS = 256
LANES = 128
PAIRS = 64
HALF = MEMBERS // 2
SLOT_CAP = 2
BRICKS = 64
FIRST = 52
ORDER = [FIRST ^ k for k in range(BRICKS)]
VMEM_LIMIT = 8 * 1024 * 1024
IDLE = 1024

DIAMETER = 0.3
SOFTENING = 0.0001
TIME_STEP = 0.02
INERTIA_SCALE = 0.05
HISTORY_DECAY = 0.9

POS = MEMBERS
ORI = MEMBERS + 3
LISTS = MEMBERS + 7
PACKED = MEMBERS + 8

LAST = (((1,), (1,)), ((), ()))
F32 = jnp.float32
BF16 = jnp.bfloat16
I32 = jnp.int32


def parts_of(value):
    high = value.astype(BF16).astype(F32)
    rest = value - high
    middle = rest.astype(BF16).astype(F32)
    return jnp.concatenate([high, middle, rest - middle], 0).astype(BF16)


def sum_parts(value):
    rows = value.shape[0] // 3
    return value[:rows] + value[rows : 2 * rows] + value[2 * rows :]


def one_hot(index_row, rows=CLUMPS):
    count = lax.broadcasted_iota(I32, (rows, index_row.shape[1]), 0)
    return jnp.where(count == index_row, 1.0, 0.0).astype(F32).astype(BF16)


def gather(parts, chosen):
    return sum_parts(jnp.dot(parts, chosen, preferred_element_type=F32))


def scatter(value, chosen):
    return sum_parts(lax.dot_general(parts_of(value), chosen, LAST, preferred_element_type=F32))


def arms_of(picked, template):
    quat = [picked[ORI + k : ORI + k + 1] for k in range(4)]
    scale = lax.rsqrt(quat[0] * quat[0] + quat[1] * quat[1] + quat[2] * quat[2] + quat[3] * quat[3])
    qw, qx, qy, qz = [q * scale for q in quat]
    matrix = [
        [1.0 - 2.0 * (qy * qy + qz * qz), 2.0 * (qx * qy - qw * qz), 2.0 * (qx * qz + qw * qy)],
        [2.0 * (qx * qy + qw * qz), 1.0 - 2.0 * (qx * qx + qz * qz), 2.0 * (qy * qz - qw * qx)],
        [2.0 * (qx * qz - qw * qy), 2.0 * (qy * qz + qw * qx), 1.0 - 2.0 * (qx * qx + qy * qy)],
    ]
    return [row[0] * template[0] + row[1] * template[1] + row[2] * template[2] for row in matrix]


def spread_template(template_ref):
    padded = jnp.concatenate([template_ref[...], jnp.zeros((5, MEMBERS), F32)], 0)
    turned = padded.T
    return [jnp.broadcast_to(turned[:, k : k + 1], (MEMBERS, LANES)) for k in range(3)]


def twice(row):
    return jnp.concatenate([row, row], 1)


def halves(value):
    lane = lax.broadcasted_iota(I32, (HALF, LANES), 1)
    return jnp.where(lane < PAIRS, value[:HALF], value[HALF:])


def place_source(src_ref, picked, arm, shift):
    for k in range(3):
        src_ref[k] = (picked[POS + k : POS + k + 1] + shift[k]) + arm[k]
    src_ref[3] = 10.0 + 10.0 * picked[0:MEMBERS]


def contact(place, weight, src_ref):
    def step(b, sums):
        other = [src_ref[k, pl.ds(b, 1), :] for k in range(4)]
        dx = place[0] - other[0]
        dy = place[1] - other[1]
        dz = place[2] - other[2]
        square = dx * dx + dy * dy + (dz * dz + SOFTENING)
        inverse = lax.rsqrt(square)
        margin = jnp.maximum(DIAMETER - square * inverse, 0.0)
        push = margin * inverse * (weight + other[3])
        return (sums[0] + push * dx, sums[1] + push * dy, sums[2] + push * dz, sums[3] + margin)

    zero = jnp.zeros((HALF, LANES), F32)
    return lax.fori_loop(0, MEMBERS, step, (zero, zero, zero, zero), unroll=16)


def body_rows(arm, force):
    turn = [
        arm[1] * force[2] - arm[2] * force[1],
        arm[2] * force[0] - arm[0] * force[2],
        arm[0] * force[1] - arm[1] * force[0],
    ]
    return jnp.concatenate(
        [jnp.sum(v, axis=0, keepdims=True) for v in list(force) + turn]
        + [jnp.zeros((2, LANES), F32)],
        0,
    )


def full_batch(picked, template, src_ref):
    arm = arms_of(picked, template)
    weight = 10.0 + 10.0 * picked[0:MEMBERS]
    tail = jnp.zeros((8, LANES), F32)
    margins = []
    for cut in (slice(0, HALF), slice(HALF, MEMBERS)):
        own = [a[cut] for a in arm]
        place = [picked[POS + k : POS + k + 1] + own[k] for k in range(3)]
        out = contact(place, weight[cut], src_ref)
        margins.append(out[3])
        tail = tail + body_rows(own, out[0:3])
    return jnp.concatenate(margins + [tail], 0)


def half_targets(picked, template):
    arm = arms_of(picked, [halves(t) for t in template])
    weight = 10.0 + 10.0 * halves(picked[0:MEMBERS])
    place = [picked[POS + k : POS + k + 1] + arm[k] for k in range(3)]
    return place, weight, arm


def half_rows(arm, out):
    lane = lax.broadcasted_iota(I32, (HALF, LANES), 1)
    lower = jnp.where(lane < PAIRS, out[3], 0.0)
    upper = jnp.where(lane < PAIRS, 0.0, out[3])
    return jnp.concatenate([lower, upper, body_rows(arm, out[0:3])], 0)


def contact_both(place, weight, src_ref, acc_ref):
    def step(b, sums):
        other = [src_ref[k, pl.ds(b, 1), :] for k in range(4)]
        offset = [place[k] - other[k] for k in range(3)]
        square = offset[0] * offset[0] + offset[1] * offset[1] + (offset[2] * offset[2] + SOFTENING)
        inverse = lax.rsqrt(square)
        margin = jnp.maximum(DIAMETER - square * inverse, 0.0)
        push = margin * inverse * (weight + other[3])
        terms = [push * d for d in offset] + [margin]
        for k in range(4):
            acc_ref[k, pl.ds(pl.multiple_of(b * 8, 8), 8), :] = jnp.sum(terms[k].reshape(HALF // 8, 8, LANES), axis=0)
        return tuple(total + term for total, term in zip(sums, terms))

    zero = jnp.zeros((HALF, LANES), F32)
    return lax.fori_loop(0, MEMBERS, step, (zero, zero, zero, zero), unroll=16)


def source_sums(acc_ref):
    out = []
    for k in range(4):
        rows = [acc_ref[k, pl.ds(r, MEMBERS, stride=8), :] for r in range(8)]
        out.append(((rows[0] + rows[1]) + (rows[2] + rows[3])) + ((rows[4] + rows[5]) + (rows[6] + rows[7])))
    return out


def place_of(brick):
    return jnp.bitwise_xor(brick, FIRST)


def in_order(rows):
    blocks = [rows[8 * k : 8 * k + 8] for k in range(BRICKS // 4)]
    return jnp.concatenate([blocks[(FIRST // 4) ^ k] for k in range(BRICKS // 4)], 0)


def routes(leaving, dest):
    to = one_hot(dest, BRICKS)
    before = lax.broadcasted_iota(I32, (PAIRS, PAIRS), 0) < lax.broadcasted_iota(I32, (PAIRS, PAIRS), 1)
    before = jnp.where(before, 1.0, 0.0).astype(BF16)
    earlier = jnp.dot(to, before, preferred_element_type=F32)
    rank = jnp.sum(earlier * to.astype(F32), axis=0, keepdims=True).astype(I32)
    column = one_hot(place_of(dest) * SLOT_CAP + rank, BRICKS * SLOT_CAP)
    leaves = one_hot(leaving)
    ones = jnp.ones((8, PAIRS), F32).astype(BF16)
    return (
        lax.dot_general(column, leaves, LAST, preferred_element_type=F32),
        lax.dot_general(ones, leaves, LAST, preferred_element_type=F32),
    )


def pack_kernel(
    pos_hbm,
    ori_hbm,
    hist_hbm,
    velocity_hbm,
    template_hbm,
    local_hbm,
    ghost_hbm,
    first_hbm,
    gap_hbm,
    leaving_hbm,
    dest_hbm,
    count_ref,
    packed_ref,
    velocity_ref,
    template_ref,
    local_ref,
    ghost_ref,
    first_ref,
    gap_ref,
    leaving_ref,
    dest_ref,
    pos_ref,
    ori_ref,
    sems,
):
    moves = [
        (hist_hbm, packed_ref.at[0:MEMBERS]),
        (pos_hbm, pos_ref),
        (ori_hbm, ori_ref),
        (local_hbm, local_ref),
        (ghost_hbm, ghost_ref),
        (leaving_hbm, leaving_ref),
        (dest_hbm, dest_ref),
        (velocity_hbm, velocity_ref),
        (template_hbm, template_ref),
        (first_hbm, first_ref),
        (gap_hbm, gap_ref),
    ]
    copies = [pltpu.make_async_copy(a, b, sems.at[k]) for k, (a, b) in enumerate(moves)]
    for copy in copies:
        copy.start()
    for copy in copies[1:]:
        copy.wait()
    live = lax.broadcasted_iota(I32, (1, PAIRS), 1) < count_ref[0]
    ghost = ghost_ref[...]
    code = jnp.where(live, ghost, ghost + IDLE)
    lists = jnp.concatenate([local_ref[...], local_ref[...], code, code], 1).astype(F32)
    packed_ref[MEMBERS:PACKED] = jnp.concatenate([pos_ref[...], ori_ref[...], lists], 0)
    copies[0].wait()


def inner_kernel(
    packed_ref,
    template_ref,
    first_ref,
    gap_ref,
    leaving_ref,
    dest_ref,
    local_ref,
    totals_ref,
    route_ref,
    departed_ref,
    spread_ref,
    target_ref,
    src_ref,
    acc_ref,
):
    template = spread_template(template_ref)
    for k in range(3):
        spread_ref[k] = template[k]
    route_ref[...], departed_ref[...] = routes(leaving_ref[...], dest_ref[...])

    own = parts_of(packed_ref[...])
    place, weight, arm = half_targets(gather(own, one_hot(twice(local_ref[...]))), template)
    for k in range(3):
        target_ref[k] = place[k]
        target_ref[4 + k] = arm[k]
    target_ref[3] = weight

    first = first_ref[...]
    second = one_hot(twice(jnp.bitwise_and(first + gap_ref[...], CLUMPS - 1)))
    first = one_hot(twice(first))
    picked = gather(own, second)
    arm_b = arms_of(picked, template)
    place_source(src_ref, picked, arm_b, (0.0, 0.0, 0.0))
    place, weight, arm = half_targets(gather(own, first), template)
    rows = half_rows(arm, contact_both(place, weight, src_ref, acc_ref))
    force_x, force_y, force_z, margin = source_sums(acc_ref)
    other = jnp.concatenate([margin, -body_rows(arm_b, (force_x, force_y, force_z))], 0)
    totals_ref[...] = scatter(rows, first) + scatter(other, second)


def before_kernel(packed_ref, inner_ref, spread_ref, brick_back_ref, slab_back_ref, totals_ref, src_ref):
    template = [spread_ref[k] for k in range(3)]
    lane = lax.broadcasted_iota(I32, (1, LANES), 1)
    low = lane < PAIRS
    brick_lists = brick_back_ref[LISTS : LISTS + 1].astype(I32)
    slab_lists = slab_back_ref[LISTS : LISTS + 1].astype(I32)
    local = jnp.where(low, brick_lists[:, :LANES], slab_lists[:, :LANES])
    code = jnp.where(low, brick_lists[:, LANES:], slab_lists[:, LANES:] - CLUMPS)
    live = (code >= 0) & (code < CLUMPS)
    before = lax.broadcasted_iota(I32, (LANES, LANES), 0) < lax.broadcasted_iota(I32, (LANES, LANES), 1)
    before = jnp.where(before, 1.0, 0.0).astype(BF16)
    flags = jnp.broadcast_to(jnp.where(live, 1.0, 0.0), (16, LANES)).astype(BF16)
    place = jnp.dot(flags, before, preferred_element_type=F32)[0:1].astype(I32)
    place = jnp.where(live, place, -1)
    count = jnp.max(place) + 1
    source = gather(parts_of(brick_back_ref[...]), one_hot(jnp.where(low, local, -1))) + gather(
        parts_of(slab_back_ref[...]), one_hot(jnp.where(low, -1, local))
    )
    target = gather(parts_of(packed_ref[...]), one_hot(jnp.bitwise_and(code, CLUMPS - 1)))
    ones = jnp.ones((1, LANES), F32)
    side = jnp.where(low, 1.0, 0.0)
    both = jnp.concatenate(
        [source[:LISTS], ones, target[:LISTS], code.astype(F32), side, jnp.zeros((7, LANES), F32)], 0
    )
    both = parts_of(both)
    totals_ref[...] = inner_ref[...]

    def batch(k, carry):
        slot = jnp.bitwise_and(lax.broadcasted_iota(I32, (LANES, LANES), 0), PAIRS - 1) + k * PAIRS
        chosen = jnp.where(slot == place, 1.0, 0.0).astype(F32).astype(BF16)
        taken = sum_parts(lax.dot_general(both, chosen, LAST, preferred_element_type=F32))
        source, target, side = taken[:PACKED], taken[PACKED : 2 * PACKED], taken[2 * PACKED : 2 * PACKED + 1]
        filled = source[LISTS : LISTS + 1]
        fill = jnp.where(lax.broadcasted_iota(I32, (PACKED, LANES), 0) == ORI, 1.0 - filled, 0.0)
        source = source + fill
        clump = jnp.where(filled > 0.5, target[LISTS:PACKED], float(IDLE)).astype(I32)
        target = target + fill
        place_source(src_ref, source, arms_of(source, template), (side - 1.0, -side, 0.0))
        spot, weight, arm = half_targets(target, template)
        rows = half_rows(arm, contact(spot, weight, src_ref))
        totals_ref[...] += scatter(rows, one_hot(clump))
        return carry

    lax.fori_loop(0, jnp.where(count > PAIRS, 2, 1), batch, 0)


def outer_kernel(
    packed_ref,
    totals_ref,
    velocity_ref,
    spread_ref,
    target_ref,
    local_ref,
    ghost_ref,
    count_ref,
    route_ref,
    brick_next_ref,
    slab_next_ref,
    state_ref,
    buffer_ref,
    src_ref,
):
    template = [spread_ref[k] for k in range(3)]
    live = lax.broadcasted_iota(I32, (1, PAIRS), 1) < count_ref[0]
    local = twice(jnp.where(live, local_ref[...], IDLE))
    ghost = twice(ghost_ref[...])
    near = ghost < CLUMPS
    source = gather(parts_of(brick_next_ref[...]), one_hot(ghost)) + gather(
        parts_of(slab_next_ref[...]), one_hot(ghost - CLUMPS)
    )
    shift = (jnp.where(near, 0.0, 1.0), jnp.where(near, 1.0, 0.0), 0.0)
    place_source(src_ref, source, arms_of(source, template), shift)
    out = contact([target_ref[k] for k in range(3)], target_ref[3], src_ref)
    rows = half_rows([target_ref[4 + k] for k in range(3)], out)
    totals = totals_ref[...] + scatter(rows, one_hot(local))

    state = packed_ref[...]
    velocity = velocity_ref[...]
    ow, ox, oy, oz = orient = [state[ORI + k : ORI + k + 1] for k in range(4)]
    linear = velocity[0:3] + TIME_STEP * totals[MEMBERS : MEMBERS + 3]
    angular = velocity[3:6] + TIME_STEP * totals[MEMBERS + 3 : MEMBERS + 6] / INERTIA_SCALE
    centre = state[POS : POS + 3] + TIME_STEP * linear
    wx, wy, wz = [angular[k : k + 1] for k in range(3)]
    spin = [
        -(wx * ox + wy * oy + wz * oz),
        ow * wx + (wy * oz - wz * oy),
        ow * wy + (wz * ox - wx * oz),
        ow * wz + (wx * oy - wy * ox),
    ]
    turned = [orient[k] + 0.5 * TIME_STEP * spin[k] for k in range(4)]
    history = HISTORY_DECAY * state[0:MEMBERS] + totals[0:MEMBERS]
    full = jnp.concatenate(
        [history, centre] + turned + [linear, angular, jnp.zeros((LANES - 77, CLUMPS), F32)], 0
    )
    state_ref[...] = full
    slots = lax.dot_general(route_ref[...].astype(BF16), parts_of(full), LAST, preferred_element_type=F32)
    buffer_ref[...] = slots[:, :LANES] + slots[:, LANES : 2 * LANES] + slots[:, 2 * LANES :]


def finish_kernel(arrived_ref, state_ref, departed_ref, staying_ref, arrivals_ref):
    departed = departed_ref[0:1] > 0.5
    staying_ref[0:13] = jnp.where(departed, 0.0, state_ref[MEMBERS : MEMBERS + 13])
    staying_ref[13:77] = jnp.where(departed, 0.0, state_ref[0:MEMBERS])
    turned = in_order(arrived_ref[...]).T
    arrivals_ref[0:13] = turned[MEMBERS : MEMBERS + 13]
    arrivals_ref[13:77] = turned[0:MEMBERS]


def vmem():
    return pl.BlockSpec(memory_space=pltpu.VMEM)


def smem():
    return pl.BlockSpec(memory_space=pltpu.SMEM)


def hbm():
    return pl.BlockSpec(memory_space=pltpu.HBM)


def small():
    return pltpu.CompilerParams(vmem_limit_bytes=VMEM_LIMIT)


def cost(flops):
    return pl.CostEstimate(flops=flops, bytes_accessed=400_000, transcendentals=flops // 30)


def array(*shape, dtype=F32):
    return jax.ShapeDtypeStruct(shape, dtype)


def from_behind(value, axis, steps):
    count = lax.axis_size(axis)
    pairs = [(source, (source + steps) % count) for source in range(count)]
    return lax.ppermute(value, axis, pairs)


def shards(
    position,
    orient,
    velocity,
    history,
    template,
    cross_local,
    cross_ghost,
    cross_count,
    inner_first,
    inner_gap,
    mig_index,
    mig_dest,
):
    lists = [v.reshape(1, PAIRS) for v in (cross_local, cross_ghost, inner_first, inner_gap, mig_index, mig_dest)]
    loads = [
        pltpu.with_memory_space_constraint(v, pltpu.HBM)
        for v in (position, orient, history, velocity, template, *lists)
    ]
    packed, velocity, template, local, ghost, first, gap, leaving, dest = pl.pallas_call(
        pack_kernel,
        out_shape=(array(PACKED, CLUMPS), array(6, CLUMPS), array(3, MEMBERS)) + (array(1, PAIRS, dtype=I32),) * 6,
        in_specs=[hbm()] * 11 + [smem()],
        out_specs=(vmem(),) * 9,
        scratch_shapes=[
            pltpu.VMEM((3, CLUMPS), F32),
            pltpu.VMEM((4, CLUMPS), F32),
            pltpu.SemaphoreType.DMA((11,)),
        ],
        compiler_params=small(),
        name="pack",
    )(*loads, cross_count)
    slab_next = from_behind(packed, "slab", -1)
    slab_back = from_behind(packed, "slab", 1)
    brick_next = from_behind(packed, "brick", -1)
    brick_back = from_behind(packed, "brick", 1)
    totals, route, departed, spread, target = pl.pallas_call(
        inner_kernel,
        out_shape=(
            array(PACKED, CLUMPS),
            array(BRICKS * SLOT_CAP, CLUMPS),
            array(8, CLUMPS),
            array(3, MEMBERS, LANES),
            array(7, HALF, LANES),
        ),
        in_specs=[vmem()] * 7,
        out_specs=(vmem(),) * 5,
        scratch_shapes=[
            pltpu.VMEM((4, MEMBERS, LANES), F32),
            pltpu.VMEM((4, 8 * MEMBERS, LANES), F32),
        ],
        cost_estimate=cost(20_000_000),
        compiler_params=small(),
        name="inner",
    )(packed, template, first, gap, leaving, dest, local)
    totals = pl.pallas_call(
        before_kernel,
        out_shape=array(PACKED, CLUMPS),
        in_specs=[vmem()] * 5,
        out_specs=vmem(),
        scratch_shapes=[pltpu.VMEM((4, MEMBERS, LANES), F32)],
        cost_estimate=cost(20_000_000),
        compiler_params=small(),
        name="before",
    )(packed, totals, spread, brick_back, slab_back)
    state, buffer = pl.pallas_call(
        outer_kernel,
        out_shape=(array(LANES, CLUMPS), array(BRICKS * SLOT_CAP, LANES)),
        in_specs=[vmem()] * 7 + [smem()] + [vmem()] * 3,
        out_specs=(vmem(),) * 2,
        scratch_shapes=[pltpu.VMEM((4, MEMBERS, LANES), F32)],
        cost_estimate=cost(15_000_000),
        compiler_params=small(),
        name="outer",
    )(
        packed,
        totals,
        velocity,
        spread,
        target,
        local,
        ghost,
        cross_count,
        route,
        brick_next,
        slab_next,
    )
    arrived = lax.all_to_all(
        buffer.reshape(BRICKS, SLOT_CAP, LANES),
        "brick",
        split_axis=0,
        concat_axis=0,
        axis_index_groups=[ORDER],
    )
    staying, arrivals = pl.pallas_call(
        finish_kernel,
        out_shape=(array(77, CLUMPS), array(77, BRICKS * SLOT_CAP)),
        in_specs=[vmem()] * 3,
        out_specs=(vmem(),) * 2,
        cost_estimate=cost(5_000_000),
        compiler_params=small(),
        name="finish",
    )(arrived.reshape(BRICKS * SLOT_CAP, LANES), state, departed)
    return (staying, arrivals)


def solution(mesh):
    both = ("slab", "brick")
    return jax.shard_map(
        shards,
        mesh=mesh,
        in_specs=(
            P(None, both),
            P(None, both),
            P(None, both),
            P(None, both),
            P(),
            P(both),
            P(both),
            P(both),
            P(both),
            P(both),
            P(both),
            P(both, None),
        ),
        out_specs=(P(None, both), P(None, both)),
        check_vma=False,
    )
```

```python
import jax
import jax.numpy as jnp
from jax import lax
from jax.experimental import pallas as pl
from jax.experimental.pallas import tpu as pltpu
from jax.sharding import PartitionSpec as P

MEMBERS = 64
CLUMPS = 256
LANES = 128
PAIRS = 64
HALF = MEMBERS // 2
SLOT_CAP = 2
BRICKS = 64
FIRST = 52
ORDER = [FIRST ^ k for k in range(BRICKS)]
VMEM_LIMIT = 8 * 1024 * 1024
IDLE = 1024

DIAMETER = 0.3
SOFTENING = 0.0001
TIME_STEP = 0.02
INERTIA_SCALE = 0.05
HISTORY_DECAY = 0.9

POS = MEMBERS
ORI = MEMBERS + 3
LISTS = MEMBERS + 7
PACKED = MEMBERS + 8

LAST = (((1,), (1,)), ((), ()))
F32 = jnp.float32
BF16 = jnp.bfloat16
I32 = jnp.int32


def parts_of(value):
    high = value.astype(BF16).astype(F32)
    rest = value - high
    middle = rest.astype(BF16).astype(F32)
    return jnp.concatenate([high, middle, rest - middle], 0).astype(BF16)


def sum_parts(value):
    rows = value.shape[0] // 3
    return value[:rows] + value[rows : 2 * rows] + value[2 * rows :]


def one_hot(index_row, rows=CLUMPS):
    count = lax.broadcasted_iota(I32, (rows, index_row.shape[1]), 0)
    return jnp.where(count == index_row, 1.0, 0.0).astype(F32).astype(BF16)


def gather(parts, chosen):
    return sum_parts(jnp.dot(parts, chosen, preferred_element_type=F32))


def scatter(value, chosen):
    return sum_parts(lax.dot_general(parts_of(value), chosen, LAST, preferred_element_type=F32))


def arms_of(picked, template):
    quat = [picked[ORI + k : ORI + k + 1] for k in range(4)]
    scale = lax.rsqrt(quat[0] * quat[0] + quat[1] * quat[1] + quat[2] * quat[2] + quat[3] * quat[3])
    qw, qx, qy, qz = [q * scale for q in quat]
    matrix = [
        [1.0 - 2.0 * (qy * qy + qz * qz), 2.0 * (qx * qy - qw * qz), 2.0 * (qx * qz + qw * qy)],
        [2.0 * (qx * qy + qw * qz), 1.0 - 2.0 * (qx * qx + qz * qz), 2.0 * (qy * qz - qw * qx)],
        [2.0 * (qx * qz - qw * qy), 2.0 * (qy * qz + qw * qx), 1.0 - 2.0 * (qx * qx + qy * qy)],
    ]
    return [row[0] * template[0] + row[1] * template[1] + row[2] * template[2] for row in matrix]


def spread_template(template_ref):
    padded = jnp.concatenate([template_ref[...], jnp.zeros((5, MEMBERS), F32)], 0)
    turned = padded.T
    return [jnp.broadcast_to(turned[:, k : k + 1], (MEMBERS, LANES)) for k in range(3)]


def twice(row):
    return jnp.concatenate([row, row], 1)


def halves(value):
    lane = lax.broadcasted_iota(I32, (HALF, LANES), 1)
    return jnp.where(lane < PAIRS, value[:HALF], value[HALF:])


def place_source(src_ref, picked, arm, shift):
    for k in range(3):
        src_ref[k] = (picked[POS + k : POS + k + 1] + shift[k]) + arm[k]
    src_ref[3] = 10.0 + 10.0 * picked[0:MEMBERS]


def contact(place, weight, src_ref):
    def step(b, sums):
        other = [src_ref[k, pl.ds(b, 1), :] for k in range(4)]
        dx = place[0] - other[0]
        dy = place[1] - other[1]
        dz = place[2] - other[2]
        square = dx * dx + dy * dy + (dz * dz + SOFTENING)
        inverse = lax.rsqrt(square)
        margin = jnp.maximum(DIAMETER - square * inverse, 0.0)
        push = margin * inverse * (weight + other[3])
        return (sums[0] + push * dx, sums[1] + push * dy, sums[2] + push * dz, sums[3] + margin)

    zero = jnp.zeros((HALF, LANES), F32)
    return lax.fori_loop(0, MEMBERS, step, (zero, zero, zero, zero), unroll=32)


def body_rows(arm, force):
    turn = [
        arm[1] * force[2] - arm[2] * force[1],
        arm[2] * force[0] - arm[0] * force[2],
        arm[0] * force[1] - arm[1] * force[0],
    ]
    return jnp.concatenate(
        [jnp.sum(v, axis=0, keepdims=True) for v in list(force) + turn]
        + [jnp.zeros((2, LANES), F32)],
        0,
    )


def full_batch(picked, template, src_ref):
    arm = arms_of(picked, template)
    weight = 10.0 + 10.0 * picked[0:MEMBERS]
    tail = jnp.zeros((8, LANES), F32)
    margins = []
    for cut in (slice(0, HALF), slice(HALF, MEMBERS)):
        own = [a[cut] for a in arm]
        place = [picked[POS + k : POS + k + 1] + own[k] for k in range(3)]
        out = contact(place, weight[cut], src_ref)
        margins.append(out[3])
        tail = tail + body_rows(own, out[0:3])
    return jnp.concatenate(margins + [tail], 0)


def half_targets(picked, template):
    arm = arms_of(picked, [halves(t) for t in template])
    weight = 10.0 + 10.0 * halves(picked[0:MEMBERS])
    place = [picked[POS + k : POS + k + 1] + arm[k] for k in range(3)]
    return place, weight, arm


def half_rows(arm, out):
    lane = lax.broadcasted_iota(I32, (HALF, LANES), 1)
    lower = jnp.where(lane < PAIRS, out[3], 0.0)
    upper = jnp.where(lane < PAIRS, 0.0, out[3])
    return jnp.concatenate([lower, upper, body_rows(arm, out[0:3])], 0)


def contact_both(place, weight, src_ref, acc_ref):
    def step(b, sums):
        other = [src_ref[k, pl.ds(b, 1), :] for k in range(4)]
        offset = [place[k] - other[k] for k in range(3)]
        square = offset[0] * offset[0] + offset[1] * offset[1] + (offset[2] * offset[2] + SOFTENING)
        inverse = lax.rsqrt(square)
        margin = jnp.maximum(DIAMETER - square * inverse, 0.0)
        push = margin * inverse * (weight + other[3])
        terms = [push * d for d in offset] + [margin]
        for k in range(4):
            acc_ref[k, pl.ds(pl.multiple_of(b * 8, 8), 8), :] = jnp.sum(terms[k].reshape(HALF // 8, 8, LANES), axis=0)
        return tuple(total + term for total, term in zip(sums, terms))

    zero = jnp.zeros((HALF, LANES), F32)
    return lax.fori_loop(0, MEMBERS, step, (zero, zero, zero, zero), unroll=32)


def source_sums(acc_ref):
    out = []
    for k in range(4):
        rows = [acc_ref[k, pl.ds(r, MEMBERS, stride=8), :] for r in range(8)]
        out.append(((rows[0] + rows[1]) + (rows[2] + rows[3])) + ((rows[4] + rows[5]) + (rows[6] + rows[7])))
    return out


def place_of(brick):
    return jnp.bitwise_xor(brick, FIRST)


def in_order(rows):
    blocks = [rows[8 * k : 8 * k + 8] for k in range(BRICKS // 4)]
    return jnp.concatenate([blocks[(FIRST // 4) ^ k] for k in range(BRICKS // 4)], 0)


def routes(leaving, dest):
    to = one_hot(dest, BRICKS)
    before = lax.broadcasted_iota(I32, (PAIRS, PAIRS), 0) < lax.broadcasted_iota(I32, (PAIRS, PAIRS), 1)
    before = jnp.where(before, 1.0, 0.0).astype(BF16)
    earlier = jnp.dot(to, before, preferred_element_type=F32)
    rank = jnp.sum(earlier * to.astype(F32), axis=0, keepdims=True).astype(I32)
    column = one_hot(place_of(dest) * SLOT_CAP + rank, BRICKS * SLOT_CAP)
    leaves = one_hot(leaving)
    ones = jnp.ones((8, PAIRS), F32).astype(BF16)
    return (
        lax.dot_general(column, leaves, LAST, preferred_element_type=F32),
        lax.dot_general(ones, leaves, LAST, preferred_element_type=F32),
    )


def pack_kernel(
    pos_hbm,
    ori_hbm,
    hist_hbm,
    velocity_hbm,
    template_hbm,
    local_hbm,
    ghost_hbm,
    first_hbm,
    gap_hbm,
    leaving_hbm,
    dest_hbm,
    count_ref,
    packed_ref,
    velocity_ref,
    template_ref,
    local_ref,
    ghost_ref,
    first_ref,
    gap_ref,
    leaving_ref,
    dest_ref,
    pos_ref,
    ori_ref,
    sems,
):
    moves = [
        (hist_hbm, packed_ref.at[0:MEMBERS]),
        (pos_hbm, pos_ref),
        (ori_hbm, ori_ref),
        (local_hbm, local_ref),
        (ghost_hbm, ghost_ref),
        (leaving_hbm, leaving_ref),
        (dest_hbm, dest_ref),
        (velocity_hbm, velocity_ref),
        (template_hbm, template_ref),
        (first_hbm, first_ref),
        (gap_hbm, gap_ref),
    ]
    copies = [pltpu.make_async_copy(a, b, sems.at[k]) for k, (a, b) in enumerate(moves)]
    for copy in copies:
        copy.start()
    for copy in copies[1:]:
        copy.wait()
    live = lax.broadcasted_iota(I32, (1, PAIRS), 1) < count_ref[0]
    ghost = ghost_ref[...]
    code = jnp.where(live, ghost, ghost + IDLE)
    lists = jnp.concatenate([local_ref[...], local_ref[...], code, code], 1).astype(F32)
    packed_ref[MEMBERS:PACKED] = jnp.concatenate([pos_ref[...], ori_ref[...], lists], 0)
    copies[0].wait()


def inner_kernel(
    packed_ref,
    template_ref,
    first_ref,
    gap_ref,
    leaving_ref,
    dest_ref,
    local_ref,
    totals_ref,
    route_ref,
    departed_ref,
    spread_ref,
    target_ref,
    src_ref,
    acc_ref,
):
    template = spread_template(template_ref)
    for k in range(3):
        spread_ref[k] = template[k]
    route_ref[...], departed_ref[...] = routes(leaving_ref[...], dest_ref[...])

    own = parts_of(packed_ref[...])
    place, weight, arm = half_targets(gather(own, one_hot(twice(local_ref[...]))), template)
    for k in range(3):
        target_ref[k] = place[k]
        target_ref[4 + k] = arm[k]
    target_ref[3] = weight

    first = first_ref[...]
    second = one_hot(twice(jnp.bitwise_and(first + gap_ref[...], CLUMPS - 1)))
    first = one_hot(twice(first))
    picked = gather(own, second)
    arm_b = arms_of(picked, template)
    place_source(src_ref, picked, arm_b, (0.0, 0.0, 0.0))
    place, weight, arm = half_targets(gather(own, first), template)
    rows = half_rows(arm, contact_both(place, weight, src_ref, acc_ref))
    force_x, force_y, force_z, margin = source_sums(acc_ref)
    other = jnp.concatenate([margin, -body_rows(arm_b, (force_x, force_y, force_z))], 0)
    totals_ref[...] = scatter(rows, first) + scatter(other, second)


def before_kernel(packed_ref, inner_ref, spread_ref, brick_back_ref, slab_back_ref, totals_ref, src_ref):
    template = [spread_ref[k] for k in range(3)]
    lane = lax.broadcasted_iota(I32, (1, LANES), 1)
    low = lane < PAIRS
    brick_lists = brick_back_ref[LISTS : LISTS + 1].astype(I32)
    slab_lists = slab_back_ref[LISTS : LISTS + 1].astype(I32)
    local = jnp.where(low, brick_lists[:, :LANES], slab_lists[:, :LANES])
    code = jnp.where(low, brick_lists[:, LANES:], slab_lists[:, LANES:] - CLUMPS)
    live = (code >= 0) & (code < CLUMPS)
    before = lax.broadcasted_iota(I32, (LANES, LANES), 0) < lax.broadcasted_iota(I32, (LANES, LANES), 1)
    before = jnp.where(before, 1.0, 0.0).astype(BF16)
    flags = jnp.broadcast_to(jnp.where(live, 1.0, 0.0), (16, LANES)).astype(BF16)
    place = jnp.dot(flags, before, preferred_element_type=F32)[0:1].astype(I32)
    place = jnp.where(live, place, -1)
    count = jnp.max(place) + 1
    source = gather(parts_of(brick_back_ref[...]), one_hot(jnp.where(low, local, -1))) + gather(
        parts_of(slab_back_ref[...]), one_hot(jnp.where(low, -1, local))
    )
    target = gather(parts_of(packed_ref[...]), one_hot(jnp.bitwise_and(code, CLUMPS - 1)))
    ones = jnp.ones((1, LANES), F32)
    side = jnp.where(low, 1.0, 0.0)
    both = jnp.concatenate(
        [source[:LISTS], ones, target[:LISTS], code.astype(F32), side, jnp.zeros((7, LANES), F32)], 0
    )
    both = parts_of(both)
    totals_ref[...] = inner_ref[...]

    def batch(k, carry):
        slot = jnp.bitwise_and(lax.broadcasted_iota(I32, (LANES, LANES), 0), PAIRS - 1) + k * PAIRS
        chosen = jnp.where(slot == place, 1.0, 0.0).astype(F32).astype(BF16)
        taken = sum_parts(lax.dot_general(both, chosen, LAST, preferred_element_type=F32))
        source, target, side = taken[:PACKED], taken[PACKED : 2 * PACKED], taken[2 * PACKED : 2 * PACKED + 1]
        filled = source[LISTS : LISTS + 1]
        fill = jnp.where(lax.broadcasted_iota(I32, (PACKED, LANES), 0) == ORI, 1.0 - filled, 0.0)
        source = source + fill
        clump = jnp.where(filled > 0.5, target[LISTS:PACKED], float(IDLE)).astype(I32)
        target = target + fill
        place_source(src_ref, source, arms_of(source, template), (side - 1.0, -side, 0.0))
        spot, weight, arm = half_targets(target, template)
        rows = half_rows(arm, contact(spot, weight, src_ref))
        totals_ref[...] += scatter(rows, one_hot(clump))
        return carry

    lax.fori_loop(0, jnp.where(count > PAIRS, 2, 1), batch, 0)


def outer_kernel(
    packed_ref,
    totals_ref,
    velocity_ref,
    spread_ref,
    target_ref,
    local_ref,
    ghost_ref,
    count_ref,
    route_ref,
    brick_next_ref,
    slab_next_ref,
    state_ref,
    buffer_ref,
    src_ref,
):
    template = [spread_ref[k] for k in range(3)]
    live = lax.broadcasted_iota(I32, (1, PAIRS), 1) < count_ref[0]
    local = twice(jnp.where(live, local_ref[...], IDLE))
    ghost = twice(ghost_ref[...])
    near = ghost < CLUMPS
    source = gather(parts_of(brick_next_ref[...]), one_hot(ghost)) + gather(
        parts_of(slab_next_ref[...]), one_hot(ghost - CLUMPS)
    )
    shift = (jnp.where(near, 0.0, 1.0), jnp.where(near, 1.0, 0.0), 0.0)
    place_source(src_ref, source, arms_of(source, template), shift)
    out = contact([target_ref[k] for k in range(3)], target_ref[3], src_ref)
    rows = half_rows([target_ref[4 + k] for k in range(3)], out)
    totals = totals_ref[...] + scatter(rows, one_hot(local))

    state = packed_ref[...]
    velocity = velocity_ref[...]
    ow, ox, oy, oz = orient = [state[ORI + k : ORI + k + 1] for k in range(4)]
    linear = velocity[0:3] + TIME_STEP * totals[MEMBERS : MEMBERS + 3]
    angular = velocity[3:6] + TIME_STEP * totals[MEMBERS + 3 : MEMBERS + 6] / INERTIA_SCALE
    centre = state[POS : POS + 3] + TIME_STEP * linear
    wx, wy, wz = [angular[k : k + 1] for k in range(3)]
    spin = [
        -(wx * ox + wy * oy + wz * oz),
        ow * wx + (wy * oz - wz * oy),
        ow * wy + (wz * ox - wx * oz),
        ow * wz + (wx * oy - wy * ox),
    ]
    turned = [orient[k] + 0.5 * TIME_STEP * spin[k] for k in range(4)]
    history = HISTORY_DECAY * state[0:MEMBERS] + totals[0:MEMBERS]
    full = jnp.concatenate(
        [history, centre] + turned + [linear, angular, jnp.zeros((LANES - 77, CLUMPS), F32)], 0
    )
    state_ref[...] = full
    slots = lax.dot_general(route_ref[...].astype(BF16), parts_of(full), LAST, preferred_element_type=F32)
    buffer_ref[...] = slots[:, :LANES] + slots[:, LANES : 2 * LANES] + slots[:, 2 * LANES :]


def finish_kernel(arrived_ref, state_ref, departed_ref, staying_ref, arrivals_ref):
    departed = departed_ref[0:1] > 0.5
    staying_ref[0:13] = jnp.where(departed, 0.0, state_ref[MEMBERS : MEMBERS + 13])
    staying_ref[13:77] = jnp.where(departed, 0.0, state_ref[0:MEMBERS])
    turned = in_order(arrived_ref[...]).T
    arrivals_ref[0:13] = turned[MEMBERS : MEMBERS + 13]
    arrivals_ref[13:77] = turned[0:MEMBERS]


def vmem():
    return pl.BlockSpec(memory_space=pltpu.VMEM)


def smem():
    return pl.BlockSpec(memory_space=pltpu.SMEM)


def hbm():
    return pl.BlockSpec(memory_space=pltpu.HBM)


def small():
    return pltpu.CompilerParams(vmem_limit_bytes=VMEM_LIMIT)


def cost(flops):
    return pl.CostEstimate(flops=flops, bytes_accessed=400_000, transcendentals=flops // 30)


def array(*shape, dtype=F32):
    return jax.ShapeDtypeStruct(shape, dtype)


def from_behind(value, axis, steps):
    count = lax.axis_size(axis)
    pairs = [(source, (source + steps) % count) for source in range(count)]
    return lax.ppermute(value, axis, pairs)


def shards(
    position,
    orient,
    velocity,
    history,
    template,
    cross_local,
    cross_ghost,
    cross_count,
    inner_first,
    inner_gap,
    mig_index,
    mig_dest,
):
    lists = [v.reshape(1, PAIRS) for v in (cross_local, cross_ghost, inner_first, inner_gap, mig_index, mig_dest)]
    loads = [
        pltpu.with_memory_space_constraint(v, pltpu.HBM)
        for v in (position, orient, history, velocity, template, *lists)
    ]
    packed, velocity, template, local, ghost, first, gap, leaving, dest = pl.pallas_call(
        pack_kernel,
        out_shape=(array(PACKED, CLUMPS), array(6, CLUMPS), array(3, MEMBERS)) + (array(1, PAIRS, dtype=I32),) * 6,
        in_specs=[hbm()] * 11 + [smem()],
        out_specs=(vmem(),) * 9,
        scratch_shapes=[
            pltpu.VMEM((3, CLUMPS), F32),
            pltpu.VMEM((4, CLUMPS), F32),
            pltpu.SemaphoreType.DMA((11,)),
        ],
        compiler_params=small(),
        name="pack",
    )(*loads, cross_count)
    slab_next = from_behind(packed, "slab", -1)
    slab_back = from_behind(packed, "slab", 1)
    brick_next = from_behind(packed, "brick", -1)
    brick_back = from_behind(packed, "brick", 1)
    totals, route, departed, spread, target = pl.pallas_call(
        inner_kernel,
        out_shape=(
            array(PACKED, CLUMPS),
            array(BRICKS * SLOT_CAP, CLUMPS),
            array(8, CLUMPS),
            array(3, MEMBERS, LANES),
            array(7, HALF, LANES),
        ),
        in_specs=[vmem()] * 7,
        out_specs=(vmem(),) * 5,
        scratch_shapes=[
            pltpu.VMEM((4, MEMBERS, LANES), F32),
            pltpu.VMEM((4, 8 * MEMBERS, LANES), F32),
        ],
        cost_estimate=cost(20_000_000),
        compiler_params=small(),
        name="inner",
    )(packed, template, first, gap, leaving, dest, local)
    totals = pl.pallas_call(
        before_kernel,
        out_shape=array(PACKED, CLUMPS),
        in_specs=[vmem()] * 5,
        out_specs=vmem(),
        scratch_shapes=[pltpu.VMEM((4, MEMBERS, LANES), F32)],
        cost_estimate=cost(20_000_000),
        compiler_params=small(),
        name="before",
    )(packed, totals, spread, brick_back, slab_back)
    state, buffer = pl.pallas_call(
        outer_kernel,
        out_shape=(array(LANES, CLUMPS), array(BRICKS * SLOT_CAP, LANES)),
        in_specs=[vmem()] * 7 + [smem()] + [vmem()] * 3,
        out_specs=(vmem(),) * 2,
        scratch_shapes=[pltpu.VMEM((4, MEMBERS, LANES), F32)],
        cost_estimate=cost(15_000_000),
        compiler_params=small(),
        name="outer",
    )(
        packed,
        totals,
        velocity,
        spread,
        target,
        local,
        ghost,
        cross_count,
        route,
        brick_next,
        slab_next,
    )
    arrived = lax.all_to_all(
        buffer.reshape(BRICKS, SLOT_CAP, LANES),
        "brick",
        split_axis=0,
        concat_axis=0,
        axis_index_groups=[ORDER],
    )
    staying, arrivals = pl.pallas_call(
        finish_kernel,
        out_shape=(array(77, CLUMPS), array(77, BRICKS * SLOT_CAP)),
        in_specs=[vmem()] * 3,
        out_specs=(vmem(),) * 2,
        cost_estimate=cost(5_000_000),
        compiler_params=small(),
        name="finish",
    )(arrived.reshape(BRICKS * SLOT_CAP, LANES), state, departed)
    return (staying, arrivals)


def solution(mesh):
    both = ("slab", "brick")
    return jax.shard_map(
        shards,
        mesh=mesh,
        in_specs=(
            P(None, both),
            P(None, both),
            P(None, both),
            P(None, both),
            P(),
            P(both),
            P(both),
            P(both),
            P(both),
            P(both),
            P(both),
            P(both, None),
        ),
        out_specs=(P(None, both), P(None, both)),
        check_vma=False,
    )
```
